32 devices in a mesh: ty: 4 (over y, core), tx: 8 (over z, x).
Axes of the slice: x: 2, y: 2, z: 4, core: 2. Of those that a mesh axis runs over, the one named last changes fastest.
Arguments:
- object_re: float32 [2048, 4096], P('ty', 'tx'), may hold values from 0.5 to 1.5
- object_im: float32 [2048, 4096], P('ty', 'tx'), may hold values from -3 to 3
- probe_re: float32 [8, 128, 128], replicated, may hold values from -2 to 2
- probe_im: float32 [8, 128, 128], replicated, may hold values from -2 to 2
- patterns: float32 [4, 8, 16, 128, 128], P('ty', 'tx'), may hold values from 0.05 to 8
- offsets: int32 [4, 8, 16, 2], P('ty', 'tx'), may hold values from 0 to 511, as said below
- counts: int32 [4, 8, 8], P('ty', 'tx'), may hold values from 0 to 2, as said below
Outputs:
- new_object_re: float32 [2048, 4096], P('ty', 'tx')
- new_object_im: float32 [2048, 4096], P('ty', 'tx')
- new_probe_re: float32 [8, 128, 128], replicated
- new_probe_im: float32 [8, 128, 128], replicated
The draws below stay inside these ranges and needn't reach their ends.
Inputs may be any that keep to these rules, and one draw needn't show every extreme that they name: Row offsets are below 512, column offsets below 512. `counts`: in every draw some reader receives 2 live scans from every owner tile of its row.
All inputs are finite; a program needn't handle non-finite values.
Results may differ from the reference program's by a relative error of at most 0.0001.
Values sent between devices are 32-bit elements; how exact they have to be, the bound alone decides.
A program may use at most 128 MiB of HBM per device.

```python
import math
import jax
import jax.numpy as jnp
from jax import lax

PATCH = 128
MODES = 8
TH = 512
TW = 512
CAP = 2
ITERS = 1
SLOTS = 16
NYO = 2048
NXO = 4096
N_TY = 4
N_TX = 8


def draw_offsets(key, part):
    key = jax.random.fold_in(key, 11)
    row_key, col_key = jax.random.split(key)
    row_values = jax.random.randint(row_key, (N_TY, N_TX, SLOTS, 1), 0, TH)
    col_values = jax.random.randint(col_key, (N_TY, N_TX, SLOTS, 1), 0, TW)
    joined = jnp.concatenate([row_values, col_values], axis=3).astype(jnp.int32)
    return joined.at[0, 0, 0].set(jnp.array([TH - 1, TW - 1], jnp.int32))


def draw_counts(key, part):
    key = jax.random.fold_in(key, 23)
    count_key, row_key, reader_key = jax.random.split(key, 3)
    drawn_counts = jax.random.randint(count_key, (N_TY, N_TX, N_TX), 0, CAP + 1)
    chosen_row = jax.random.randint(row_key, (), 0, N_TY)
    chosen_reader = jax.random.randint(reader_key, (), 0, N_TX)
    row_ids = jnp.arange(N_TY, dtype=jnp.int32)[:, None, None]
    reader_ids = jnp.arange(N_TX, dtype=jnp.int32)[None, None, :]
    picked = (row_ids == chosen_row) & (reader_ids == chosen_reader)
    return jnp.where(picked, CAP, drawn_counts).astype(jnp.int32)


def shard_levels(own_key, shape, cuts, low, largest):
    def one(dim, parts):
        heights = jax.random.uniform(jax.random.fold_in(jax.random.fold_in(own_key, 6), dim), (parts,), jnp.float32, low / len(cuts), largest / len(cuts))
        return jnp.repeat(jnp.exp(heights), shape[dim] // parts).reshape((-1,) + (1,) * (len(shape) - dim - 1))

    level = one(*cuts[0])
    for cut in cuts[1:]:
        level = level * one(*cut)
    return level


def centred(stream_key, extent, deviation, limit, pieces=(), kind=jnp.bfloat16):
    loudness = shard_levels(stream_key, extent, pieces, -0.22, 0.18) if pieces else 1.0
    values = jax.random.normal(stream_key, extent, jnp.float32) * deviation * loudness
    return jnp.minimum(jnp.maximum(values, -limit), limit).astype(kind)


def setup_inputs(seed: int = 0) -> dict:
    keys = jax.random.split(jax.random.key(seed), 8)
    return {
        "object_re": jnp.clip(0.5 + 1.0 * jax.random.uniform(keys[0], (NYO, NXO), jnp.float32) ** shard_levels(keys[0], (NYO, NXO), ((0, 4), (1, 8)), -0.2, 0.2), 0.5, 1.5),
        "object_im": centred(keys[1], (NYO, NXO), 0.5, 3.0, ((0, 4), (1, 8)), jnp.float32),
        "probe_re": centred(keys[2], (MODES, PATCH, PATCH), 0.3, 2.0, (), jnp.float32),
        "probe_im": centred(keys[3], (MODES, PATCH, PATCH), 0.3, 2.0, (), jnp.float32),
        "patterns": jnp.clip(jnp.exp(math.log(8.0) - 5.075174 * jax.random.uniform(keys[4], (N_TY, N_TX, SLOTS, PATCH, PATCH), jnp.float32) ** shard_levels(keys[4], (N_TY, N_TX, SLOTS, PATCH, PATCH), ((0, 4), (1, 8)), -0.2, 0.2)), 0.05, 8.0),
        "offsets": draw_offsets(jax.random.fold_in(keys[7], 71), 0),
        "counts": draw_counts(jax.random.fold_in(keys[7], 71), 0),
    }


def residual_wave(probe_real, probe_imag, patch_real, patch_imag, pattern):
    exit_real = probe_real * patch_real - probe_imag * patch_imag
    exit_imag = probe_real * patch_imag + probe_imag * patch_real
    far_field = jnp.fft.fft2(lax.complex(exit_real, exit_imag), norm='ortho')
    total_power = lax.optimization_barrier(jnp.sum(far_field.real * far_field.real + far_field.imag * far_field.imag, axis=0))
    factor = jnp.sqrt(pattern) / jnp.sqrt(jnp.maximum(total_power, 1.0)) - 1.0
    back_wave = jnp.fft.ifft2(far_field * factor[None], norm='ortho')
    return (back_wave.real, back_wave.imag)

def add_patch(target, piece_add, corner):
    current = lax.dynamic_slice(target, corner, piece_add.shape)
    return lax.dynamic_update_slice(target, current + piece_add, corner)

def reference(object_re, object_im, probe_re, probe_im, patterns, offsets, counts):
    owner_row = jnp.arange(N_TY, dtype=jnp.int32)[:, None, None, None]
    owner_col = jnp.arange(N_TX, dtype=jnp.int32)[None, :, None, None]
    reader = jnp.arange(N_TX, dtype=jnp.int32)[None, None, :, None]
    within = jnp.arange(CAP, dtype=jnp.int32)[None, None, None, :]
    grouped = offsets.reshape(N_TY, N_TX, N_TX, CAP, 2)
    row_starts = (owner_row * TH + grouped[..., 0]).reshape(-1).astype(jnp.int32)
    col_starts = (owner_col * TW + grouped[..., 1]).reshape(-1).astype(jnp.int32)
    alive_flags = (within < counts[:, :, :, None]).astype(jnp.float32).reshape(-1)
    pattern_index = ((owner_row * N_TX + reader) * SLOTS + owner_col * CAP + within).reshape(-1).astype(jnp.int32)
    flat_patterns = patterns.reshape(N_TY * N_TX * SLOTS, PATCH, PATCH)
    object_real, object_imag = (object_re, object_im)
    probe_real, probe_imag = (probe_re, probe_im)
    for iteration in range(ITERS):
        padded_real = jnp.pad(object_real, ((0, PATCH), (0, PATCH)))
        padded_imag = jnp.pad(object_imag, ((0, PATCH), (0, PATCH)))
        probe_power = lax.optimization_barrier(jnp.sum(probe_real * probe_real + probe_imag * probe_imag, axis=0))

        def visit_scan(running, element):
            numer_real, numer_imag, illumination, grad_real, grad_imag, object_norm = running
            row_start, col_start, alive_flag, chosen = element
            corner = (row_start, col_start)
            patch_real = lax.dynamic_slice(padded_real, corner, (PATCH, PATCH)) * alive_flag
            patch_imag = lax.dynamic_slice(padded_imag, corner, (PATCH, PATCH)) * alive_flag
            chi_real, chi_imag = residual_wave(probe_real, probe_imag, patch_real, patch_imag, flat_patterns[chosen])
            update_real = lax.optimization_barrier(jnp.sum(probe_real * chi_real + probe_imag * chi_imag, axis=0))
            update_imag = lax.optimization_barrier(jnp.sum(probe_real * chi_imag - probe_imag * chi_real, axis=0))
            numer_real = add_patch(numer_real, update_real, corner)
            numer_imag = add_patch(numer_imag, update_imag, corner)
            illumination = add_patch(illumination, probe_power * alive_flag, corner)
            grad_real = grad_real + patch_real * chi_real + patch_imag * chi_imag
            grad_imag = grad_imag + patch_real * chi_imag - patch_imag * chi_real
            object_norm = object_norm + patch_real * patch_real + patch_imag * patch_imag
            return ((numer_real, numer_imag, illumination, grad_real, grad_imag, object_norm), None)
        plane = jnp.zeros((NYO + PATCH, NXO + PATCH), jnp.float32)
        modal = jnp.zeros((MODES, PATCH, PATCH), jnp.float32)
        initial = (plane, plane, plane, modal, modal, jnp.zeros((PATCH, PATCH), jnp.float32))
        result, unused = lax.scan(visit_scan, initial, (row_starts, col_starts, alive_flags, pattern_index))
        numer_real, numer_imag, illumination, grad_real, grad_imag, object_norm = result
        denominator = illumination[:NYO, :NXO] + 0.1 * jnp.max(probe_power)
        object_real = object_real + numer_real[:NYO, :NXO] / denominator
        object_imag = object_imag + numer_imag[:NYO, :NXO] / denominator
        probe_real = probe_real + grad_real / (object_norm + 1.0)
        probe_imag = probe_imag + grad_imag / (object_norm + 1.0)
    return (object_real, object_imag, probe_real, probe_imag)
```

```python
import math

import jax
import jax.numpy as jnp
import ml_dtypes
import numpy as np
from jax import lax
from jax.experimental import pallas as pl
from jax.experimental.pallas import tpu as pltpu
from jax.sharding import PartitionSpec as P

BF16 = jnp.bfloat16
F32 = jnp.float32
LANES = 128


def from_behind(value, axis, steps):
    count = lax.axis_size(axis)
    first, last = (max(0, -steps), min(count, count - steps))
    return lax.ppermute(value, axis, [(source, source + steps) for source in range(first, last)])


def dft_tables(extent):
    k = np.arange(extent)
    angle = (k[:, None] * k[None, :] % extent) * (-2.0 * math.pi / extent)
    cos, sin = np.cos(angle) / math.sqrt(extent), np.sin(angle) / math.sqrt(extent)
    table = np.block([[cos, sin], [-sin, cos]])

    def parts(values):
        high = values.astype(np.float32).astype(ml_dtypes.bfloat16)
        low = (values - high.astype(np.float64)).astype(np.float32).astype(ml_dtypes.bfloat16)
        return high, low

    high, low = parts(table)
    flip_high, flip_low = parts(table.T)
    return (
        np.concatenate([high, high, low], axis=0),
        np.concatenate([flip_high, flip_high, flip_low], axis=1),
        np.concatenate([high, high, low], axis=1),
        np.concatenate([flip_high, flip_high, flip_low], axis=0),
    )


def split(value):
    high = value.astype(BF16)
    low = (value - high.astype(F32)).astype(BF16)
    return high, low


def right_product(real, imag, table):
    rh, rl = split(real)
    ih, il = split(imag)
    lhs = jnp.concatenate([rh, ih, rl, il, rh, ih], axis=1)
    return jnp.dot(lhs, table, preferred_element_type=F32)


def left_product(table, real, imag):
    rh, rl = split(real)
    ih, il = split(imag)
    rhs = jnp.concatenate([rh, ih, rl, il, rh, ih], axis=0)
    return jnp.dot(table, rhs, preferred_element_type=F32)


def main_kernel(
    offsets, counts, wide_re, wide_im, probe_re, probe_im, measured,
    right_fwd, left_fwd, left_inv, right_inv,
    numer_re, numer_im, illum, grads,
    patch, power, far, update,
):
    slots, extent = measured.shape[0], measured.shape[1]
    modes = probe_re.shape[0]
    capacity = slots // counts.shape[0]
    numer_re[...] = jnp.zeros_like(numer_re)
    numer_im[...] = jnp.zeros_like(numer_im)
    illum[...] = jnp.zeros_like(illum)
    grads[...] = jnp.zeros_like(grads)
    lane = lax.broadcasted_iota(jnp.int32, (extent, LANES), 1)
    summed = probe_re[0] * probe_re[0] + probe_im[0] * probe_im[0]
    for m in range(1, modes):
        summed = summed + probe_re[m] * probe_re[m] + probe_im[m] * probe_im[m]
    power[...] = summed

    def visit(slot, carry):
        alive = slot % capacity < counts[slot // capacity]

        @pl.when(alive)
        def _():
            row = offsets[slot, 0]
            col = offsets[slot, 1]
            block = col // LANES
            inner = col % LANES
            rows = pl.ds(row, extent)
            back = lax.rem(LANES - inner, LANES)

            def cut(wide):
                first = pltpu.roll(wide[block, rows, :], back, 1)
                second = pltpu.roll(wide[block + 1, rows, :], back, 1)
                return jnp.where(lane < LANES - inner, first, second)

            patch[0] = cut(wide_re)
            patch[1] = cut(wide_im)
            total = jnp.zeros((extent, extent), F32)
            for m in range(0, modes, 2):
                mids = []
                for n in (m, m + 1):
                    a, b = patch[0], patch[1]
                    p, q = probe_re[n], probe_im[n]
                    mids.append(right_product(p * a - q * b, p * b + q * a, right_fwd[...]))
                wide_real = jnp.concatenate([y[:, :extent] for y in mids], axis=1)
                wide_imag = jnp.concatenate([y[:, extent:] for y in mids], axis=1)
                z = left_product(left_fwd[...], wide_real, wide_imag)
                far[m // 2] = z
                s = z[:extent] * z[:extent] + z[extent:] * z[extent:]
                total = total + s[:, :extent] + s[:, extent:]
            factor = jnp.sqrt(measured[slot]) / jnp.sqrt(jnp.maximum(total, 1.0)) - 1.0
            both = jnp.concatenate([factor, factor], axis=1)
            up_re = jnp.zeros((extent, extent), F32)
            up_im = jnp.zeros((extent, extent), F32)
            for m in range(0, modes, 2):
                z = far[m // 2]
                g = left_product(left_inv[...], z[:extent] * both, z[extent:] * both)
                for n in (m, m + 1):
                    cut_n = slice((n - m) * extent, (n - m + 1) * extent)
                    chi = right_product(g[:extent, cut_n], g[extent:, cut_n], right_inv[...])
                    c, d = chi[:, :extent], chi[:, extent:]
                    a, b = patch[0], patch[1]
                    p, q = probe_re[n], probe_im[n]
                    up_re = up_re + p * c + q * d
                    up_im = up_im + p * d - q * c
                    grads[n] += a * c + b * d
                    grads[modes + n] += a * d - b * c
            a, b = patch[0], patch[1]
            grads[2 * modes] += a * a + b * b

            def place(target, piece):
                moved = pltpu.roll(piece, inner, 1)
                target[block, rows, :] += jnp.where(lane >= inner, moved, 0.0)
                target[block + 1, rows, :] += jnp.where(lane < inner, moved, 0.0)

            place(numer_re, up_re)
            place(numer_im, up_im)
            place(illum, power[...])

        return carry

    lax.fori_loop(0, slots, visit, 0)


def local_work(offsets, counts, wide_re, wide_im, probe_re, probe_im, measured):
    modes, extent = probe_re.shape[0], probe_re.shape[1]
    tables = dft_tables(extent)
    vmem = pl.BlockSpec(memory_space=pltpu.VMEM)
    smem = pl.BlockSpec(memory_space=pltpu.SMEM)
    plane = jax.ShapeDtypeStruct(wide_re.shape, F32)
    return pl.pallas_call(
        main_kernel,
        out_shape=(plane, plane, plane, jax.ShapeDtypeStruct((2 * modes + 1, extent, extent), F32)),
        in_specs=[smem, smem] + [vmem] * 9,
        out_specs=(vmem,) * 4,
        scratch_shapes=[
            pltpu.VMEM((2, extent, extent), F32),
            pltpu.VMEM((extent, extent), F32),
            pltpu.VMEM((modes // 2, 2 * extent, 2 * extent), F32),
            pltpu.VMEM((2, extent, extent), F32),
        ],
        compiler_params=pltpu.CompilerParams(vmem_limit_bytes=48 * 1024 * 1024),
        name="local_work",
    )(offsets, counts, wide_re, wide_im, probe_re, probe_im, measured, *tables)


def blocked(value):
    rows, cols = value.shape
    return value.reshape(rows, cols // LANES, LANES).transpose(1, 0, 2)


def unblocked(value):
    blocks, rows, lanes = value.shape
    return value.transpose(1, 0, 2).reshape(rows, blocks * lanes)


def body(object_re, object_im, probe_re, probe_im, patterns, offsets, counts):
    height, tile_width = object_re.shape
    extent = probe_re.shape[1]
    measured = lax.all_to_all(patterns[0, 0], "tx", split_axis=0, concat_axis=0, tiled=True)
    right_rim = from_behind((object_re[:, :extent], object_im[:, :extent]), "tx", -1)
    wide_real = jnp.concatenate([object_re, right_rim[0]], axis=1)
    wide_imag = jnp.concatenate([object_im, right_rim[1]], axis=1)
    lower_rim = from_behind((wide_real[:extent], wide_imag[:extent]), "ty", -1)
    extended_real = jnp.concatenate([wide_real, lower_rim[0]], axis=0)
    extended_imag = jnp.concatenate([wide_imag, lower_rim[1]], axis=0)
    numer_real, numer_imag, illumination, grads = local_work(
        offsets[0, 0], counts[0, 0], blocked(extended_real), blocked(extended_imag),
        probe_re, probe_im, measured,
    )
    numer_real, numer_imag, illumination = (
        unblocked(numer_real), unblocked(numer_imag), unblocked(illumination)
    )
    probe_power = jnp.sum(probe_re * probe_re + probe_im * probe_im, axis=0)
    below = from_behind((numer_real[height:], numer_imag[height:], illumination[height:]), "ty", 1)
    upper_real = numer_real[:height].at[:extent].add(below[0])
    upper_imag = numer_imag[:height].at[:extent].add(below[1])
    upper_illum = illumination[:height].at[:extent].add(below[2])
    beside = from_behind(
        (upper_real[:, tile_width:], upper_imag[:, tile_width:], upper_illum[:, tile_width:]),
        "tx",
        1,
    )
    final_real = upper_real[:, :tile_width].at[:, :extent].add(beside[0])
    final_imag = upper_imag[:, :tile_width].at[:, :extent].add(beside[1])
    final_illum = upper_illum[:, :tile_width].at[:, :extent].add(beside[2])
    denominator = final_illum + 0.1 * jnp.max(probe_power)
    object_re = object_re + final_real / denominator
    object_im = object_im + final_imag / denominator
    summed = lax.psum(grads, ("ty", "tx"))
    modes = probe_re.shape[0]
    norm = summed[2 * modes] + 1.0
    probe_re = probe_re + summed[:modes] / norm
    probe_im = probe_im + summed[modes : 2 * modes] / norm
    return (object_re, object_im, probe_re, probe_im)


def solution(mesh):
    return jax.shard_map(
        body,
        mesh=mesh,
        in_specs=(
            P("ty", "tx"),
            P("ty", "tx"),
            P(),
            P(),
            P("ty", "tx", None, None, None),
            P("ty", "tx", None, None),
            P("ty", "tx", None),
        ),
        out_specs=(P("ty", "tx"), P("ty", "tx"), P(), P()),
        check_vma=False,
    )
```

```python
import math

import jax
import jax.numpy as jnp
import ml_dtypes
import numpy as np
from jax import lax
from jax.experimental import pallas as pl
from jax.experimental.pallas import tpu as pltpu
from jax.sharding import PartitionSpec as P

BF16 = jnp.bfloat16
F32 = jnp.float32
LANES = 128


def dft_tables(extent):
    k = np.arange(extent)
    angle = (k[:, None] * k[None, :] % extent) * (-2.0 * math.pi / extent)
    cos, sin = np.cos(angle) / math.sqrt(extent), np.sin(angle) / math.sqrt(extent)
    table = np.block([[cos, sin], [-sin, cos]])

    def parts(values):
        high = values.astype(np.float32).astype(ml_dtypes.bfloat16)
        low = (values - high.astype(np.float64)).astype(np.float32).astype(ml_dtypes.bfloat16)
        return high, low

    high, low = parts(table)
    flip_high, flip_low = parts(table.T)
    return (
        np.concatenate([high, high, low], axis=0),
        np.concatenate([flip_high, flip_high, flip_low], axis=1),
        np.concatenate([high, high, low], axis=1),
        np.concatenate([flip_high, flip_high, flip_low], axis=0),
    )


def split(value):
    high = value.astype(BF16)
    low = (value - high.astype(F32)).astype(BF16)
    return high, low


def right_product(real, imag, table):
    rh, rl = split(real)
    ih, il = split(imag)
    lhs = jnp.concatenate([rh, ih, rl, il, rh, ih], axis=1)
    return jnp.dot(lhs, table, preferred_element_type=F32)


def left_product(table, real, imag):
    rh, rl = split(real)
    ih, il = split(imag)
    rhs = jnp.concatenate([rh, ih, rl, il, rh, ih], axis=0)
    return jnp.dot(table, rhs, preferred_element_type=F32)


def main_kernel(
    offsets, counts, wide_re, wide_im, probe_re, probe_im, measured,
    right_fwd, left_fwd, left_inv, right_inv,
    numer, grads,
    patch, power, far,
):
    slots, extent = measured.shape[0], measured.shape[1]
    modes = probe_re.shape[0]
    capacity = slots // counts.shape[0]
    numer[...] = jnp.zeros_like(numer)
    grads[...] = jnp.zeros_like(grads)
    lane = lax.broadcasted_iota(jnp.int32, (extent, LANES), 1)
    summed = probe_re[0] * probe_re[0] + probe_im[0] * probe_im[0]
    for m in range(1, modes):
        summed = summed + probe_re[m] * probe_re[m] + probe_im[m] * probe_im[m]
    power[...] = summed

    def visit(slot, carry):
        alive = slot % capacity < counts[slot // capacity]

        @pl.when(alive)
        def _():
            row = offsets[slot, 0]
            col = offsets[slot, 1]
            block = col // LANES
            inner = col % LANES
            rows = pl.ds(row, extent)
            back = lax.rem(LANES - inner, LANES)

            def cut(wide):
                first = pltpu.roll(wide[block, rows, :], back, 1)
                second = pltpu.roll(wide[block + 1, rows, :], back, 1)
                return jnp.where(lane < LANES - inner, first, second)

            patch[0] = cut(wide_re)
            patch[1] = cut(wide_im)
            total = jnp.zeros((extent, extent), F32)
            for m in range(0, modes, 2):
                mids = []
                for n in (m, m + 1):
                    a, b = patch[0], patch[1]
                    p, q = probe_re[n], probe_im[n]
                    mids.append(right_product(p * a - q * b, p * b + q * a, right_fwd[...]))
                wide_real = jnp.concatenate([y[:, :extent] for y in mids], axis=1)
                wide_imag = jnp.concatenate([y[:, extent:] for y in mids], axis=1)
                z = left_product(left_fwd[...], wide_real, wide_imag)
                far[m // 2] = z
                s = z[:extent] * z[:extent] + z[extent:] * z[extent:]
                total = total + s[:, :extent] + s[:, extent:]
            factor = jnp.sqrt(measured[slot]) / jnp.sqrt(jnp.maximum(total, 1.0)) - 1.0
            both = jnp.concatenate([factor, factor], axis=1)
            up_re = jnp.zeros((extent, extent), F32)
            up_im = jnp.zeros((extent, extent), F32)
            for m in range(0, modes, 2):
                z = far[m // 2]
                g = left_product(left_inv[...], z[:extent] * both, z[extent:] * both)
                for n in (m, m + 1):
                    cut_n = slice((n - m) * extent, (n - m + 1) * extent)
                    chi = right_product(g[:extent, cut_n], g[extent:, cut_n], right_inv[...])
                    c, d = chi[:, :extent], chi[:, extent:]
                    a, b = patch[0], patch[1]
                    p, q = probe_re[n], probe_im[n]
                    up_re = up_re + p * c + q * d
                    up_im = up_im + p * d - q * c
                    grads[n] += a * c + b * d
                    grads[modes + n] += a * d - b * c
            a, b = patch[0], patch[1]
            grads[2 * modes] += a * a + b * b

            def place(plane, piece):
                moved = pltpu.roll(piece, inner, 1)
                numer[plane, block, rows, :] += jnp.where(lane >= inner, moved, 0.0)
                numer[plane, block + 1, rows, :] += jnp.where(lane < inner, moved, 0.0)

            place(0, up_re)
            place(1, up_im)
            place(2, power[...])

        return carry

    lax.fori_loop(0, slots, visit, 0)


def local_work(
    offsets, counts, wide_re, wide_im, probe_re, probe_im, measured, grad_planes
):
    modes, extent = probe_re.shape[0], probe_re.shape[1]
    tables = dft_tables(extent)
    vmem = pl.BlockSpec(memory_space=pltpu.VMEM)
    smem = pl.BlockSpec(memory_space=pltpu.SMEM)
    return pl.pallas_call(
        main_kernel,
        out_shape=(
            jax.ShapeDtypeStruct((3,) + wide_re.shape, F32),
            jax.ShapeDtypeStruct((grad_planes, extent, extent), F32),
        ),
        in_specs=[smem, smem] + [vmem] * 9,
        out_specs=(vmem,) * 2,
        scratch_shapes=[
            pltpu.VMEM((2, extent, extent), F32),
            pltpu.VMEM((extent, extent), F32),
            pltpu.VMEM((modes // 2, 2 * extent, 2 * extent), F32),
        ],
        compiler_params=pltpu.CompilerParams(vmem_limit_bytes=48 * 1024 * 1024),
        name="local_work",
    )(offsets, counts, wide_re, wide_im, probe_re, probe_im, measured, *tables)


def greet(partners):
    barrier = pltpu.get_barrier_semaphore()
    for partner in partners:
        pl.semaphore_signal(barrier, inc=1, device_id=partner, device_id_type=pl.DeviceIdType.MESH)
    pl.semaphore_wait(barrier, len(partners))


def remote(src, dst, send, recv, partner):
    return pltpu.make_async_remote_copy(
        src_ref=src, dst_ref=dst, send_sem=send, recv_sem=recv,
        device_id=partner, device_id_type=pl.DeviceIdType.MESH,
    )


def first_exchange_kernel(
    n_ty, n_tx, obj_re, obj_im, patterns, wide_re, wide_im, measured,
    rim_send, rim_recv, scan_send, scan_recv, own_sem,
):
    ty, tx = lax.axis_index("ty"), lax.axis_index("tx")
    height, width = obj_re.shape
    extent = patterns.shape[1]
    blocks = width // LANES
    capacity = patterns.shape[0] // n_tx
    up, down = lax.rem(ty + n_ty - 1, n_ty), lax.rem(ty + 1, n_ty)
    left, right = lax.rem(tx + n_tx - 1, n_tx), lax.rem(tx + 1, n_tx)
    peers = [lax.rem(tx + d, n_tx) for d in range(1, n_tx)]
    greet(
        [(ty, p) for p in peers]
        + [(up, tx), (down, tx), (up, left), (down, right)]
    )
    rims = []
    for plane, (obj, wide) in enumerate(((obj_re, wide_re), (obj_im, wide_im))):
        base = plane * (blocks + 2)
        top = pl.ds(0, extent)
        below = pl.ds(height, extent)
        rims.append((
            obj.at[:, pl.ds(0, LANES)], wide.at[blocks, pl.ds(0, height), :], base,
            (ty, left), tx > 0, tx < n_tx - 1,
        ))
        for b in range(blocks):
            rims.append((
                obj.at[top, pl.ds(b * LANES, LANES)], wide.at[b, below, :], base + 1 + b,
                (up, tx), ty > 0, ty < n_ty - 1,
            ))
        rims.append((
            obj.at[top, pl.ds(0, LANES)], wide.at[blocks, below, :], base + 1 + blocks,
            (up, left), jnp.logical_and(tx > 0, ty > 0),
            jnp.logical_and(tx < n_tx - 1, ty < n_ty - 1),
        ))

    for src, dst, sem, partner, sends, takes in rims:
        @pl.when(sends)
        def _():
            remote(src, dst, rim_send.at[sem], rim_recv.at[sem], partner).start()

    def scan_copy(d):
        peer = peers[d - 1]
        return remote(
            patterns.at[pl.ds(peer * capacity, capacity)],
            measured.at[pl.ds(tx * capacity, capacity)],
            scan_send.at[d - 1], scan_recv.at[d - 1], (ty, peer),
        )

    for d in range(1, n_tx):
        scan_copy(d).start()
    own = pl.ds(tx * capacity, capacity)
    own_copy = pltpu.make_async_copy(patterns.at[own], measured.at[own], own_sem)
    own_copy.start()
    for obj, wide in ((obj_re, wide_re), (obj_im, wide_im)):
        for b in range(blocks):
            wide[b, :height, :] = obj[:, b * LANES : (b + 1) * LANES]
        for dst, absent in (
            (wide.at[blocks, pl.ds(0, height), :], tx == n_tx - 1),
            (wide.at[pl.ds(0, blocks), pl.ds(height, extent), :], ty == n_ty - 1),
            (
                wide.at[blocks, pl.ds(height, extent), :],
                jnp.logical_or(tx == n_tx - 1, ty == n_ty - 1),
            ),
        ):
            @pl.when(absent)
            def _():
                dst[...] = jnp.zeros(dst.shape, F32)

    own_copy.wait()
    for src, dst, sem, partner, sends, takes in rims:
        @pl.when(sends)
        def _():
            remote(src, dst, rim_send.at[sem], rim_recv.at[sem], partner).wait_send()

        @pl.when(takes)
        def _():
            remote(src, dst, rim_send.at[sem], rim_recv.at[sem], partner).wait_recv()

    for d in range(1, n_tx):
        source = lax.rem(tx + n_tx - d, n_tx)
        scan_copy(d).wait_send()
        remote(
            patterns.at[pl.ds(source * capacity, capacity)],
            measured.at[pl.ds(source * capacity, capacity)],
            scan_send.at[d - 1], scan_recv.at[d - 1], (ty, source),
        ).wait_recv()


def first_exchange(n_ty, n_tx, obj_re, obj_im, patterns):
    height, width = obj_re.shape
    extent = patterns.shape[1]
    blocks = width // LANES
    vmem = pl.BlockSpec(memory_space=pltpu.VMEM)
    wide = jax.ShapeDtypeStruct((blocks + 1, height + extent, LANES), F32)
    count = 2 * (blocks + 2)
    return pl.pallas_call(
        lambda *refs: first_exchange_kernel(n_ty, n_tx, *refs),
        out_shape=(wide, wide, jax.ShapeDtypeStruct(patterns.shape, F32)),
        in_specs=[vmem] * 3,
        out_specs=(vmem,) * 3,
        scratch_shapes=[
            pltpu.SemaphoreType.DMA((count,)),
            pltpu.SemaphoreType.DMA((count,)),
            pltpu.SemaphoreType.DMA((n_tx - 1,)),
            pltpu.SemaphoreType.DMA((n_tx - 1,)),
            pltpu.SemaphoreType.DMA,
        ],
        compiler_params=pltpu.CompilerParams(
            collective_id=0, has_side_effects=True, vmem_limit_bytes=48 * 1024 * 1024
        ),
        name="comm_first",
    )(obj_re, obj_im, patterns)


def stages_of(n_ty, n_tx):
    wanted = [("ty", 1, 2), ("ty", 2, n_ty // 2), ("tx", 1, 2), ("tx", 2, n_tx // 2)]
    return [stage for stage in wanted if stage[2] > 1]


def last_exchange_kernel(
    n_ty, n_tx, modes, numer, grads, obj_re, obj_im, probe_re, probe_im,
    new_re, new_im, new_probe_re, new_probe_im,
    beside, below, corner, result, halo_send, halo_recv, *scratch,
):
    stages = stages_of(n_ty, n_tx)
    depth = len(stages)
    received = scratch[:depth]
    partial = scratch[depth : 2 * depth - 1]
    send_sems, recv_sems, back_send, back_recv = scratch[2 * depth - 1 :]
    ty, tx = lax.axis_index("ty"), lax.axis_index("tx")
    height, width = obj_re.shape
    extent = probe_re.shape[1]
    blocks = width // LANES
    up, down = lax.rem(ty + n_ty - 1, n_ty), lax.rem(ty + 1, n_ty)
    left, right = lax.rem(tx + n_tx - 1, n_tx), lax.rem(tx + 1, n_tx)

    def member(stage):
        axis, stride, size = stage
        return lax.rem((ty if axis == "ty" else tx) // stride, size)

    def peer(stage, shift):
        axis, stride, size = stage
        q = member(stage)
        other = lax.rem(q + shift + size, size)
        if axis == "ty":
            return other, (ty + (other - q) * stride, tx)
        return other, (ty, tx + (other - q) * stride)

    partners = [(ty, left), (ty, right), (up, tx), (down, tx), (up, left), (down, right)]
    for stage in stages:
        for d in range(1, stage[2]):
            partners.append(peer(stage, d)[1])
    greet(partners)

    halos = (
        (numer.at[:, blocks, pl.ds(0, height), :], beside, 0, (ty, right),
         tx < n_tx - 1, tx > 0),
        (numer.at[:, pl.ds(0, blocks), pl.ds(height, extent), :], below, 1, (down, tx),
         ty < n_ty - 1, ty > 0),
        (numer.at[:, blocks, pl.ds(height, extent), :], corner, 2, (down, right),
         jnp.logical_and(tx < n_tx - 1, ty < n_ty - 1), jnp.logical_and(tx > 0, ty > 0)),
    )

    def halo_copy(halo):
        src, dst, sem, partner = halo[:4]
        return remote(src, dst, halo_send.at[sem], halo_recv.at[sem], partner)

    def start_halos():
        for halo in halos:
            @pl.when(halo[4])
            def _():
                halo_copy(halo).start()

    rows = grads.shape[0]
    lengths = [rows]
    for stage in stages:
        lengths.append(lengths[-1] // stage[2])
    firsts = [0]
    while len(firsts) <= depth:
        firsts.append(firsts[-1] + (stages[len(firsts) - 1][2] - 1))
    source = grads
    base = jnp.int32(0)
    for s, stage in enumerate(stages):
        length = lengths[s + 1]
        copies = []
        for d in range(1, stage[2]):
            other, device = peer(stage, d)
            sem = firsts[s] + d - 1
            copies.append(remote(
                source.at[pl.ds(pl.multiple_of(other * length, 8), length), :],
                received[s].at[d - 1],
                send_sems.at[sem], recv_sems.at[sem], device,
            ))
        for copy in copies:
            copy.start()
        if s == 0:
            start_halos()
        for copy in copies:
            copy.wait()
        q = member(stage)
        total = source[pl.ds(pl.multiple_of(q * length, 8), length), :]
        for d in range(1, stage[2]):
            total = total + received[s][d - 1]
        base = base + q * length
        if s < depth - 1:
            source = partial[s]
            source[...] = total
        else:
            result[pl.ds(pl.multiple_of(base, 8), length), :] = total
    pending = []
    for s in range(depth - 1, -1, -1):
        stage, length = stages[s], lengths[s + 1]
        held = result.at[pl.ds(pl.multiple_of(base, 8), length), :]
        copies = []
        for d in range(1, stage[2]):
            other, device = peer(stage, d)
            sem = firsts[s] + d - 1
            copy = remote(held, held, back_send.at[sem], back_recv.at[sem], device)
            copy.start()
            copies.append(copy)
        q = member(stage)
        for d in range(1, stage[2]):
            other, device = peer(stage, -d)
            sem = firsts[s] + d - 1
            place = result.at[pl.ds(pl.multiple_of(base + (other - q) * length, 8), length), :]
            remote(place, place, back_send.at[sem], back_recv.at[sem], device).wait_recv()
        pending += copies
        base = base - q * length
    for copy in pending:
        copy.wait_send()

    norm = result[pl.ds(2 * modes * extent, extent), :] + 1.0
    for m in range(modes):
        real = result[pl.ds(m * extent, extent), :]
        imag = result[pl.ds((modes + m) * extent, extent), :]
        new_probe_re[m] = probe_re[m] + real / norm
        new_probe_im[m] = probe_im[m] + imag / norm

    for halo in halos:
        @pl.when(halo[4])
        def _():
            halo_copy(halo).wait_send()

        @pl.when(halo[5])
        def _():
            halo_copy(halo).wait_recv()

    for halo in halos:
        @pl.when(jnp.logical_not(halo[5]))
        def _():
            halo[1][...] = jnp.zeros(halo[1].shape, F32)

    power = probe_re[0] * probe_re[0] + probe_im[0] * probe_im[0]
    for m in range(1, modes):
        power = power + probe_re[m] * probe_re[m] + probe_im[m] * probe_im[m]
    floor = 0.1 * jnp.max(power)
    for b in range(blocks):
        cols = slice(b * LANES, (b + 1) * LANES)
        for r in range(0, height, extent):
            band = slice(r, r + extent)
            sums = []
            for plane in range(3):
                value = numer[plane, b, band, :]
                if r == 0:
                    value = value + below[plane, b]
                if b == 0:
                    value = value + beside[plane, band, :]
                if r == 0 and b == 0:
                    value = value + corner[plane]
                sums.append(value)
            weight = sums[2] + floor
            new_re[band, cols] = obj_re[band, cols] + sums[0] / weight
            new_im[band, cols] = obj_im[band, cols] + sums[1] / weight


def last_exchange(n_ty, n_tx, numer, grads, obj_re, obj_im, probe_re, probe_im):
    modes, extent = probe_re.shape[0], probe_re.shape[1]
    height, width = obj_re.shape
    blocks = width // LANES
    stages = stages_of(n_ty, n_tx)
    rows = grads.shape[0]
    vmem = pl.BlockSpec(memory_space=pltpu.VMEM)
    received, partial = [], []
    length = rows
    for stage in stages:
        length = length // stage[2]
        received.append(pltpu.VMEM((stage[2] - 1, length, LANES), F32))
        partial.append(pltpu.VMEM((length, LANES), F32))
    count = sum(stage[2] - 1 for stage in stages)
    tile = jax.ShapeDtypeStruct(obj_re.shape, F32)
    wave = jax.ShapeDtypeStruct(probe_re.shape, F32)
    return pl.pallas_call(
        lambda *refs: last_exchange_kernel(n_ty, n_tx, modes, *refs),
        out_shape=(tile, tile, wave, wave),
        in_specs=[vmem] * 6,
        out_specs=(vmem,) * 4,
        scratch_shapes=[
            pltpu.VMEM((3, height, LANES), F32),
            pltpu.VMEM((3, blocks, extent, LANES), F32),
            pltpu.VMEM((3, extent, LANES), F32),
            pltpu.VMEM((rows, LANES), F32),
            pltpu.SemaphoreType.DMA((3,)),
            pltpu.SemaphoreType.DMA((3,)),
            *received,
            *partial[:-1],
            *[pltpu.SemaphoreType.DMA((count,))] * 4,
        ],
        compiler_params=pltpu.CompilerParams(
            collective_id=1, has_side_effects=True, vmem_limit_bytes=48 * 1024 * 1024
        ),
        name="comm_last",
    )(numer, grads, obj_re, obj_im, probe_re, probe_im)


def body(object_re, object_im, probe_re, probe_im, patterns, offsets, counts):
    n_ty, n_tx = lax.axis_size("ty"), lax.axis_size("tx")
    modes, extent = probe_re.shape[0], probe_re.shape[1]
    wide_re, wide_im, measured = first_exchange(n_ty, n_tx, object_re, object_im, patterns[0, 0])
    rows = (2 * modes + 1) * extent
    unit = 8 * n_ty * n_tx
    unit = unit * extent // math.gcd(unit, extent)
    grad_planes = -(-rows // unit) * unit // extent
    numer, grads = local_work(
        offsets[0, 0], counts[0, 0], wide_re, wide_im, probe_re, probe_im, measured, grad_planes
    )
    return last_exchange(
        n_ty, n_tx, numer, grads.reshape(grad_planes * extent, extent),
        object_re, object_im, probe_re, probe_im,
    )


def solution(mesh):
    return jax.shard_map(
        body,
        mesh=mesh,
        in_specs=(
            P("ty", "tx"),
            P("ty", "tx"),
            P(),
            P(),
            P("ty", "tx", None, None, None),
            P("ty", "tx", None, None),
            P("ty", "tx", None),
        ),
        out_specs=(P("ty", "tx"), P("ty", "tx"), P(), P()),
        check_vma=False,
    )
```

```python
import math

import jax
import jax.numpy as jnp
import ml_dtypes
import numpy as np
from jax import lax
from jax.experimental import pallas as pl
from jax.experimental.pallas import tpu as pltpu
from jax.sharding import PartitionSpec as P

BF16 = jnp.bfloat16
F32 = jnp.float32
LANES = 128


def dft_tables(extent):
    k = np.arange(extent)
    angle = (k[:, None] * k[None, :] % extent) * (-2.0 * math.pi / extent)
    cos, sin = np.cos(angle) / math.sqrt(extent), np.sin(angle) / math.sqrt(extent)
    table = np.block([[cos, sin], [-sin, cos]])

    def parts(values):
        high = values.astype(np.float32).astype(ml_dtypes.bfloat16)
        low = (values - high.astype(np.float64)).astype(np.float32).astype(ml_dtypes.bfloat16)
        return high, low

    high, low = parts(table)
    flip_high, flip_low = parts(table.T)
    return (
        np.concatenate([high, high, low], axis=0),
        np.concatenate([flip_high, flip_high, flip_low], axis=0),
    )


def split(value):
    high = value.astype(BF16)
    low = (value - high.astype(F32)).astype(BF16)
    return high, low


def right_product(real, imag, table):
    rh, rl = split(real)
    ih, il = split(imag)
    lhs = jnp.concatenate([rh, ih, rl, il, rh, ih], axis=1)
    return jnp.dot(lhs, table, preferred_element_type=F32)


def alive(counts, slot, capacity):
    return lax.rem(slot, capacity) < counts[slot // capacity]


def cut_patch(offsets, slot, wide_re, wide_im, extent, patch):
    row, col = offsets[slot, 0], offsets[slot, 1]
    block, inner = col // LANES, lax.rem(col, LANES)
    rows = pl.ds(row, extent)
    back = lax.rem(LANES - inner, LANES)
    lane = lax.broadcasted_iota(jnp.int32, (extent, LANES), 1)
    for plane, wide in enumerate((wide_re, wide_im)):
        first = pltpu.roll(wide[block, rows, :], back, 1)
        second = pltpu.roll(wide[block + 1, rows, :], back, 1)
        patch[plane] = jnp.where(lane < LANES - inner, first, second)


def forward_kernel(
    capacity, offsets, counts, wide_re, wide_im, probe_re, probe_im, table,
    far, power_seen, patch,
):
    slot = pl.program_id(0)
    modes, extent = probe_re.shape[0], probe_re.shape[1]

    @pl.when(alive(counts, slot, capacity))
    def _():
        cut_patch(offsets, slot, wide_re, wide_im, extent, patch)
        total = jnp.zeros((extent, extent), F32)
        for n in range(modes):
            a, b = patch[0], patch[1]
            p, q = probe_re[n], probe_im[n]
            y = right_product(p * a - q * b, p * b + q * a, table[...])
            z = right_product(y[:, :extent].T, y[:, extent:].T, table[...])
            far[0, n] = z
            s = z * z
            total = total + s[:, :extent] + s[:, extent:]
        power_seen[0] = total


def backward_kernel(
    capacity, offsets, counts, wide_re, wide_im, probe_re, probe_im, table,
    far, power_seen, measured, numer, grads, patch, power,
):
    slot = pl.program_id(0)
    modes, extent = probe_re.shape[0], probe_re.shape[1]

    @pl.when(slot == 0)
    def _():
        numer[...] = jnp.zeros_like(numer)
        grads[...] = jnp.zeros_like(grads)
        summed = probe_re[0] * probe_re[0] + probe_im[0] * probe_im[0]
        for m in range(1, modes):
            summed = summed + probe_re[m] * probe_re[m] + probe_im[m] * probe_im[m]
        power[...] = summed

    @pl.when(alive(counts, slot, capacity))
    def _():
        cut_patch(offsets, slot, wide_re, wide_im, extent, patch)
        row, col = offsets[slot, 0], offsets[slot, 1]
        block, inner = col // LANES, lax.rem(col, LANES)
        rows = pl.ds(row, extent)
        lane = lax.broadcasted_iota(jnp.int32, (extent, LANES), 1)
        seen = jnp.sqrt(jnp.maximum(power_seen[0], 1.0))
        factor = jnp.sqrt(measured[0].T) / seen - 1.0
        up_re = jnp.zeros((extent, extent), F32)
        up_im = jnp.zeros((extent, extent), F32)
        for n in range(modes):
            z = far[0, n]
            y = right_product(z[:, :extent] * factor, z[:, extent:] * factor, table[...])
            chi = right_product(y[:, :extent].T, y[:, extent:].T, table[...])
            c, d = chi[:, :extent], chi[:, extent:]
            a, b = patch[0], patch[1]
            p, q = probe_re[n], probe_im[n]
            up_re = up_re + p * c + q * d
            up_im = up_im + p * d - q * c
            grads[n] += a * c + b * d
            grads[modes + n] += a * d - b * c
        a, b = patch[0], patch[1]
        grads[2 * modes] += a * a + b * b

        def place(plane, piece):
            moved = pltpu.roll(piece, inner, 1)
            numer[plane, block, rows, :] += jnp.where(lane >= inner, moved, 0.0)
            numer[plane, block + 1, rows, :] += jnp.where(lane < inner, moved, 0.0)

        place(0, up_re)
        place(1, up_im)
        place(2, power[...])


def forward(capacity, offsets, counts, wide_re, wide_im, probe_re, probe_im, table):
    slots = offsets.shape[0]
    modes, extent = probe_re.shape[0], probe_re.shape[1]
    vmem = pl.BlockSpec(memory_space=pltpu.VMEM)
    smem = pl.BlockSpec(memory_space=pltpu.SMEM)
    return pl.pallas_call(
        lambda *refs: forward_kernel(capacity, *refs),
        grid=(slots,),
        out_shape=(
            jax.ShapeDtypeStruct((slots, modes, extent, 2 * extent), F32),
            jax.ShapeDtypeStruct((slots, extent, extent), F32),
        ),
        in_specs=[smem, smem] + [vmem] * 5,
        out_specs=(
            pl.BlockSpec((1, modes, extent, 2 * extent), lambda i: (i, 0, 0, 0)),
            pl.BlockSpec((1, extent, extent), lambda i: (i, 0, 0)),
        ),
        scratch_shapes=[pltpu.VMEM((2, extent, extent), F32)],
        compiler_params=pltpu.CompilerParams(vmem_limit_bytes=40 * 1024 * 1024),
        cost_estimate=pl.CostEstimate(
            flops=slots * modes * 24 * extent**3, bytes_accessed=slots * modes * extent**2 * 8,
            transcendentals=0,
        ),
        name="local_forward",
    )(offsets, counts, wide_re, wide_im, probe_re, probe_im, table)


def backward(
    capacity, grad_planes, offsets, counts, wide_re, wide_im, probe_re, probe_im, table,
    far, power_seen, measured,
):
    slots = offsets.shape[0]
    modes, extent = probe_re.shape[0], probe_re.shape[1]
    vmem = pl.BlockSpec(memory_space=pltpu.VMEM)
    smem = pl.BlockSpec(memory_space=pltpu.SMEM)
    return pl.pallas_call(
        lambda *refs: backward_kernel(capacity, *refs),
        grid=(slots,),
        out_shape=(
            jax.ShapeDtypeStruct((3,) + wide_re.shape, F32),
            jax.ShapeDtypeStruct((grad_planes, extent, extent), F32),
        ),
        in_specs=[smem, smem] + [vmem] * 5 + [
            pl.BlockSpec((1, modes, extent, 2 * extent), lambda i: (i, 0, 0, 0)),
            pl.BlockSpec((1, extent, extent), lambda i: (i, 0, 0)),
            pl.BlockSpec((1, extent, extent), lambda i: (i, 0, 0)),
        ],
        out_specs=(vmem,) * 2,
        scratch_shapes=[
            pltpu.VMEM((2, extent, extent), F32),
            pltpu.VMEM((extent, extent), F32),
        ],
        compiler_params=pltpu.CompilerParams(vmem_limit_bytes=48 * 1024 * 1024),
        cost_estimate=pl.CostEstimate(
            flops=slots * modes * 24 * extent**3, bytes_accessed=slots * modes * extent**2 * 8,
            transcendentals=0,
        ),
        name="local_backward",
    )(offsets, counts, wide_re, wide_im, probe_re, probe_im, table, far, power_seen, measured)


def greet(partners):
    barrier = pltpu.get_barrier_semaphore()
    for partner in partners:
        pl.semaphore_signal(barrier, inc=1, device_id=partner, device_id_type=pl.DeviceIdType.MESH)
    pl.semaphore_wait(barrier, len(partners))


def remote(src, dst, send, recv, partner):
    return pltpu.make_async_remote_copy(
        src_ref=src, dst_ref=dst, send_sem=send, recv_sem=recv,
        device_id=partner, device_id_type=pl.DeviceIdType.MESH,
    )


def first_exchange_kernel(
    n_ty, n_tx, extent, obj_re, obj_im, wide_re, wide_im, rim_send, rim_recv,
):
    ty, tx = lax.axis_index("ty"), lax.axis_index("tx")
    height, width = obj_re.shape
    blocks = width // LANES
    up, down = lax.rem(ty + n_ty - 1, n_ty), lax.rem(ty + 1, n_ty)
    left, right = lax.rem(tx + n_tx - 1, n_tx), lax.rem(tx + 1, n_tx)
    greet([(ty, left), (ty, right), (up, tx), (down, tx), (up, left), (down, right)])
    rims = []
    for plane, (obj, wide) in enumerate(((obj_re, wide_re), (obj_im, wide_im))):
        base = plane * (blocks + 2)
        top = pl.ds(0, extent)
        below = pl.ds(height, extent)
        rims.append((
            obj.at[:, pl.ds(0, LANES)], wide.at[blocks, pl.ds(0, height), :], base,
            (ty, left), tx > 0, tx < n_tx - 1,
        ))
        for b in range(blocks):
            rims.append((
                obj.at[top, pl.ds(b * LANES, LANES)], wide.at[b, below, :], base + 1 + b,
                (up, tx), ty > 0, ty < n_ty - 1,
            ))
        rims.append((
            obj.at[top, pl.ds(0, LANES)], wide.at[blocks, below, :], base + 1 + blocks,
            (up, left), jnp.logical_and(tx > 0, ty > 0),
            jnp.logical_and(tx < n_tx - 1, ty < n_ty - 1),
        ))

    for src, dst, sem, partner, sends, takes in rims:
        @pl.when(sends)
        def _():
            remote(src, dst, rim_send.at[sem], rim_recv.at[sem], partner).start()

    for obj, wide in ((obj_re, wide_re), (obj_im, wide_im)):
        for b in range(blocks):
            wide[b, :height, :] = obj[:, b * LANES : (b + 1) * LANES]
        for dst, absent in (
            (wide.at[blocks, pl.ds(0, height), :], tx == n_tx - 1),
            (wide.at[pl.ds(0, blocks), pl.ds(height, extent), :], ty == n_ty - 1),
            (
                wide.at[blocks, pl.ds(height, extent), :],
                jnp.logical_or(tx == n_tx - 1, ty == n_ty - 1),
            ),
        ):
            @pl.when(absent)
            def _():
                dst[...] = jnp.zeros(dst.shape, F32)

    for src, dst, sem, partner, sends, takes in rims:
        @pl.when(sends)
        def _():
            remote(src, dst, rim_send.at[sem], rim_recv.at[sem], partner).wait_send()

        @pl.when(takes)
        def _():
            remote(src, dst, rim_send.at[sem], rim_recv.at[sem], partner).wait_recv()


def first_exchange(n_ty, n_tx, extent, obj_re, obj_im):
    height, width = obj_re.shape
    blocks = width // LANES
    vmem = pl.BlockSpec(memory_space=pltpu.VMEM)
    wide = jax.ShapeDtypeStruct((blocks + 1, height + extent, LANES), F32)
    count = 2 * (blocks + 2)
    return pl.pallas_call(
        lambda *refs: first_exchange_kernel(n_ty, n_tx, extent, *refs),
        out_shape=(wide, wide),
        in_specs=[vmem] * 2,
        out_specs=(vmem,) * 2,
        scratch_shapes=[
            pltpu.SemaphoreType.DMA((count,)),
            pltpu.SemaphoreType.DMA((count,)),
        ],
        compiler_params=pltpu.CompilerParams(
            collective_id=0, has_side_effects=True, vmem_limit_bytes=48 * 1024 * 1024
        ),
        name="comm_first",
    )(obj_re, obj_im)


def stages_of(n_ty, n_tx):
    wanted = [("ty", 1, 2), ("ty", 2, n_ty // 2), ("tx", 1, 2), ("tx", 2, n_tx // 2)]
    return [stage for stage in wanted if stage[2] > 1]


def last_exchange_kernel(
    n_ty, n_tx, modes, numer, grads, obj_re, obj_im, probe_re, probe_im,
    new_re, new_im, new_probe_re, new_probe_im,
    beside, below, corner, result, halo_send, halo_recv, *scratch,
):
    stages = stages_of(n_ty, n_tx)
    depth = len(stages)
    received = scratch[:depth]
    partial = scratch[depth : 2 * depth - 1]
    send_sems, recv_sems, back_send, back_recv = scratch[2 * depth - 1 :]
    ty, tx = lax.axis_index("ty"), lax.axis_index("tx")
    height, width = obj_re.shape
    extent = probe_re.shape[1]
    blocks = width // LANES
    up, down = lax.rem(ty + n_ty - 1, n_ty), lax.rem(ty + 1, n_ty)
    left, right = lax.rem(tx + n_tx - 1, n_tx), lax.rem(tx + 1, n_tx)

    def member(stage):
        axis, stride, size = stage
        return lax.rem((ty if axis == "ty" else tx) // stride, size)

    def peer(stage, shift):
        axis, stride, size = stage
        q = member(stage)
        other = lax.rem(q + shift + size, size)
        if axis == "ty":
            return other, (ty + (other - q) * stride, tx)
        return other, (ty, tx + (other - q) * stride)

    partners = [(ty, left), (ty, right), (up, tx), (down, tx), (up, left), (down, right)]
    for stage in stages:
        for d in range(1, stage[2]):
            partners.append(peer(stage, d)[1])
    greet(partners)

    halos = (
        (numer.at[:, blocks, pl.ds(0, height), :], beside, 0, (ty, right),
         tx < n_tx - 1, tx > 0),
        (numer.at[:, pl.ds(0, blocks), pl.ds(height, extent), :], below, 1, (down, tx),
         ty < n_ty - 1, ty > 0),
        (numer.at[:, blocks, pl.ds(height, extent), :], corner, 2, (down, right),
         jnp.logical_and(tx < n_tx - 1, ty < n_ty - 1), jnp.logical_and(tx > 0, ty > 0)),
    )

    def halo_copy(halo):
        src, dst, sem, partner = halo[:4]
        return remote(src, dst, halo_send.at[sem], halo_recv.at[sem], partner)

    def start_halos():
        for halo in halos:
            @pl.when(halo[4])
            def _():
                halo_copy(halo).start()

    rows = grads.shape[0]
    lengths = [rows]
    for stage in stages:
        lengths.append(lengths[-1] // stage[2])
    firsts = [0]
    while len(firsts) <= depth:
        firsts.append(firsts[-1] + (stages[len(firsts) - 1][2] - 1))
    source = grads
    base = jnp.int32(0)
    for s, stage in enumerate(stages):
        length = lengths[s + 1]
        copies = []
        for d in range(1, stage[2]):
            other, device = peer(stage, d)
            sem = firsts[s] + d - 1
            copies.append(remote(
                source.at[pl.ds(pl.multiple_of(other * length, 8), length), :],
                received[s].at[d - 1],
                send_sems.at[sem], recv_sems.at[sem], device,
            ))
        for copy in copies:
            copy.start()
        if s == 0:
            start_halos()
        for copy in copies:
            copy.wait()
        q = member(stage)
        total = source[pl.ds(pl.multiple_of(q * length, 8), length), :]
        for d in range(1, stage[2]):
            total = total + received[s][d - 1]
        base = base + q * length
        if s < depth - 1:
            source = partial[s]
            source[...] = total
        else:
            result[pl.ds(pl.multiple_of(base, 8), length), :] = total
    pending = []
    for s in range(depth - 1, -1, -1):
        stage, length = stages[s], lengths[s + 1]
        held = result.at[pl.ds(pl.multiple_of(base, 8), length), :]
        copies = []
        for d in range(1, stage[2]):
            other, device = peer(stage, d)
            sem = firsts[s] + d - 1
            copy = remote(held, held, back_send.at[sem], back_recv.at[sem], device)
            copy.start()
            copies.append(copy)
        q = member(stage)
        for d in range(1, stage[2]):
            other, device = peer(stage, -d)
            sem = firsts[s] + d - 1
            place = result.at[pl.ds(pl.multiple_of(base + (other - q) * length, 8), length), :]
            remote(place, place, back_send.at[sem], back_recv.at[sem], device).wait_recv()
        pending += copies
        base = base - q * length
    for copy in pending:
        copy.wait_send()

    norm = result[pl.ds(2 * modes * extent, extent), :] + 1.0
    for m in range(modes):
        real = result[pl.ds(m * extent, extent), :]
        imag = result[pl.ds((modes + m) * extent, extent), :]
        new_probe_re[m] = probe_re[m] + real / norm
        new_probe_im[m] = probe_im[m] + imag / norm

    for halo in halos:
        @pl.when(halo[4])
        def _():
            halo_copy(halo).wait_send()

        @pl.when(halo[5])
        def _():
            halo_copy(halo).wait_recv()

    for halo in halos:
        @pl.when(jnp.logical_not(halo[5]))
        def _():
            halo[1][...] = jnp.zeros(halo[1].shape, F32)

    power = probe_re[0] * probe_re[0] + probe_im[0] * probe_im[0]
    for m in range(1, modes):
        power = power + probe_re[m] * probe_re[m] + probe_im[m] * probe_im[m]
    floor = 0.1 * jnp.max(power)
    for b in range(blocks):
        cols = slice(b * LANES, (b + 1) * LANES)
        for r in range(0, height, extent):
            band = slice(r, r + extent)
            sums = []
            for plane in range(3):
                value = numer[plane, b, band, :]
                if r == 0:
                    value = value + below[plane, b]
                if b == 0:
                    value = value + beside[plane, band, :]
                if r == 0 and b == 0:
                    value = value + corner[plane]
                sums.append(value)
            weight = sums[2] + floor
            new_re[band, cols] = obj_re[band, cols] + sums[0] / weight
            new_im[band, cols] = obj_im[band, cols] + sums[1] / weight


def last_exchange(n_ty, n_tx, numer, grads, obj_re, obj_im, probe_re, probe_im):
    modes, extent = probe_re.shape[0], probe_re.shape[1]
    height, width = obj_re.shape
    blocks = width // LANES
    stages = stages_of(n_ty, n_tx)
    rows = grads.shape[0]
    vmem = pl.BlockSpec(memory_space=pltpu.VMEM)
    received, partial = [], []
    length = rows
    for stage in stages:
        length = length // stage[2]
        received.append(pltpu.VMEM((stage[2] - 1, length, LANES), F32))
        partial.append(pltpu.VMEM((length, LANES), F32))
    count = sum(stage[2] - 1 for stage in stages)
    tile = jax.ShapeDtypeStruct(obj_re.shape, F32)
    wave = jax.ShapeDtypeStruct(probe_re.shape, F32)
    return pl.pallas_call(
        lambda *refs: last_exchange_kernel(n_ty, n_tx, modes, *refs),
        out_shape=(tile, tile, wave, wave),
        in_specs=[vmem] * 6,
        out_specs=(vmem,) * 4,
        scratch_shapes=[
            pltpu.VMEM((3, height, LANES), F32),
            pltpu.VMEM((3, blocks, extent, LANES), F32),
            pltpu.VMEM((3, extent, LANES), F32),
            pltpu.VMEM((rows, LANES), F32),
            pltpu.SemaphoreType.DMA((3,)),
            pltpu.SemaphoreType.DMA((3,)),
            *received,
            *partial[:-1],
            *[pltpu.SemaphoreType.DMA((count,))] * 4,
        ],
        compiler_params=pltpu.CompilerParams(
            collective_id=1, has_side_effects=True, vmem_limit_bytes=48 * 1024 * 1024
        ),
        name="comm_last",
    )(numer, grads, obj_re, obj_im, probe_re, probe_im)


def body(object_re, object_im, probe_re, probe_im, patterns, offsets, counts):
    n_ty, n_tx = lax.axis_size("ty"), lax.axis_size("tx")
    modes, extent = probe_re.shape[0], probe_re.shape[1]
    measured = lax.all_to_all(patterns[0, 0], "tx", split_axis=0, concat_axis=0, tiled=True)
    wide_re, wide_im = first_exchange(n_ty, n_tx, extent, object_re, object_im)
    rows = (2 * modes + 1) * extent
    unit = 8 * n_ty * n_tx
    unit = unit * extent // math.gcd(unit, extent)
    grad_planes = -(-rows // unit) * unit // extent
    capacity = patterns.shape[2] // n_tx
    table, back_table = dft_tables(extent)
    shared = (offsets[0, 0], counts[0, 0], wide_re, wide_im, probe_re, probe_im)
    far, power_seen = forward(capacity, *shared, table)
    numer, grads = backward(
        capacity, grad_planes, *shared, back_table, far, power_seen, measured
    )
    return last_exchange(
        n_ty, n_tx, numer, grads.reshape(grad_planes * extent, extent),
        object_re, object_im, probe_re, probe_im,
    )


def solution(mesh):
    return jax.shard_map(
        body,
        mesh=mesh,
        in_specs=(
            P("ty", "tx"),
            P("ty", "tx"),
            P(),
            P(),
            P("ty", "tx", None, None, None),
            P("ty", "tx", None, None),
            P("ty", "tx", None),
        ),
        out_specs=(P("ty", "tx"), P("ty", "tx"), P(), P()),
        check_vma=False,
    )
```

```python
import math

import jax
import jax.numpy as jnp
import ml_dtypes
import numpy as np
from jax import lax
from jax.experimental import pallas as pl
from jax.experimental.pallas import tpu as pltpu
from jax.sharding import PartitionSpec as P

BF16 = jnp.bfloat16
F32 = jnp.float32
LANES = 128


def dft_tables(extent):
    k = np.arange(extent)
    angle = (k[:, None] * k[None, :] % extent) * (-2.0 * math.pi / extent)
    cos, sin = np.cos(angle) / math.sqrt(extent), np.sin(angle) / math.sqrt(extent)
    table = np.block([[cos, sin], [-sin, cos]])

    def parts(values):
        high = values.astype(np.float32).astype(ml_dtypes.bfloat16)
        low = (values - high.astype(np.float64)).astype(np.float32).astype(ml_dtypes.bfloat16)
        return high, low

    high, low = parts(table)
    flip_high, flip_low = parts(table.T)
    return (
        np.concatenate([high, high, low], axis=0),
        np.concatenate([flip_high, flip_high, flip_low], axis=1),
        np.concatenate([high, high, low], axis=1),
        np.concatenate([flip_high, flip_high, flip_low], axis=0),
    )


def split(value):
    high = value.astype(BF16)
    low = (value - high.astype(F32)).astype(BF16)
    return high, low


def right_product(real, imag, table):
    rh, rl = split(real)
    ih, il = split(imag)
    lhs = jnp.concatenate([rh, ih, rl, il, rh, ih], axis=1)
    return jnp.dot(lhs, table, preferred_element_type=F32)


def left_product(table, real, imag):
    rh, rl = split(real)
    ih, il = split(imag)
    rhs = jnp.concatenate([rh, ih, rl, il, rh, ih], axis=0)
    return jnp.dot(table, rhs, preferred_element_type=F32)


def main_kernel(
    offsets, counts, wide_re, wide_im, probe_re, probe_im, measured,
    right_fwd, left_fwd, left_inv, right_inv,
    numer, grads,
    patch, power, far,
):
    slots, extent = measured.shape[0], measured.shape[1]
    modes = probe_re.shape[0]
    capacity = slots // counts.shape[0]
    numer[...] = jnp.zeros_like(numer)
    grads[...] = jnp.zeros_like(grads)
    lane = lax.broadcasted_iota(jnp.int32, (extent, LANES), 1)
    summed = probe_re[0] * probe_re[0] + probe_im[0] * probe_im[0]
    for m in range(1, modes):
        summed = summed + probe_re[m] * probe_re[m] + probe_im[m] * probe_im[m]
    power[...] = summed

    def visit(slot, carry):
        alive = slot % capacity < counts[slot // capacity]

        @pl.when(alive)
        def _():
            row = offsets[slot, 0]
            col = offsets[slot, 1]
            block = col // LANES
            inner = col % LANES
            rows = pl.ds(row, extent)
            back = lax.rem(LANES - inner, LANES)

            def cut(wide):
                first = pltpu.roll(wide[block, rows, :], back, 1)
                second = pltpu.roll(wide[block + 1, rows, :], back, 1)
                return jnp.where(lane < LANES - inner, first, second)

            patch[0] = cut(wide_re)
            patch[1] = cut(wide_im)
            total = jnp.zeros((extent, extent), F32)
            for m in range(0, modes, 2):
                mids = []
                for n in (m, m + 1):
                    a, b = patch[0], patch[1]
                    p, q = probe_re[n], probe_im[n]
                    mids.append(right_product(p * a - q * b, p * b + q * a, right_fwd[...]))
                wide_real = jnp.concatenate([y[:, :extent] for y in mids], axis=1)
                wide_imag = jnp.concatenate([y[:, extent:] for y in mids], axis=1)
                z = left_product(left_fwd[...], wide_real, wide_imag)
                far[m // 2] = z
                s = z[:extent] * z[:extent] + z[extent:] * z[extent:]
                total = total + s[:, :extent] + s[:, extent:]
            factor = jnp.sqrt(measured[slot]) / jnp.sqrt(jnp.maximum(total, 1.0)) - 1.0
            both = jnp.concatenate([factor, factor], axis=1)
            up_re = jnp.zeros((extent, extent), F32)
            up_im = jnp.zeros((extent, extent), F32)
            for m in range(0, modes, 2):
                z = far[m // 2]
                g = left_product(left_inv[...], z[:extent] * both, z[extent:] * both)
                for n in (m, m + 1):
                    cut_n = slice((n - m) * extent, (n - m + 1) * extent)
                    chi = right_product(g[:extent, cut_n], g[extent:, cut_n], right_inv[...])
                    c, d = chi[:, :extent], chi[:, extent:]
                    a, b = patch[0], patch[1]
                    p, q = probe_re[n], probe_im[n]
                    up_re = up_re + p * c + q * d
                    up_im = up_im + p * d - q * c
                    grads[n] += a * c + b * d
                    grads[modes + n] += a * d - b * c
            a, b = patch[0], patch[1]
            grads[2 * modes] += a * a + b * b

            def place(plane, piece):
                moved = pltpu.roll(piece, inner, 1)
                numer[plane, block, rows, :] += jnp.where(lane >= inner, moved, 0.0)
                numer[plane, block + 1, rows, :] += jnp.where(lane < inner, moved, 0.0)

            place(0, up_re)
            place(1, up_im)
            place(2, power[...])

        return carry

    lax.fori_loop(0, slots, visit, 0)


def local_work(
    offsets, counts, wide_re, wide_im, probe_re, probe_im, measured, grad_planes
):
    modes, extent = probe_re.shape[0], probe_re.shape[1]
    tables = dft_tables(extent)
    vmem = pl.BlockSpec(memory_space=pltpu.VMEM)
    smem = pl.BlockSpec(memory_space=pltpu.SMEM)
    return pl.pallas_call(
        main_kernel,
        out_shape=(
            jax.ShapeDtypeStruct((3,) + wide_re.shape, F32),
            jax.ShapeDtypeStruct((grad_planes, extent, extent), F32),
        ),
        in_specs=[smem, smem] + [vmem] * 9,
        out_specs=(vmem,) * 2,
        scratch_shapes=[
            pltpu.VMEM((2, extent, extent), F32),
            pltpu.VMEM((extent, extent), F32),
            pltpu.VMEM((modes // 2, 2 * extent, 2 * extent), F32),
        ],
        compiler_params=pltpu.CompilerParams(vmem_limit_bytes=48 * 1024 * 1024),
        name="local_work",
    )(offsets, counts, wide_re, wide_im, probe_re, probe_im, measured, *tables)


def greet(partners):
    barrier = pltpu.get_barrier_semaphore()
    for partner in partners:
        pl.semaphore_signal(barrier, inc=1, device_id=partner, device_id_type=pl.DeviceIdType.MESH)
    pl.semaphore_wait(barrier, len(partners))


def remote(src, dst, send, recv, partner):
    return pltpu.make_async_remote_copy(
        src_ref=src, dst_ref=dst, send_sem=send, recv_sem=recv,
        device_id=partner, device_id_type=pl.DeviceIdType.MESH,
    )


def first_exchange_kernel(
    n_ty, n_tx, obj_re, obj_im, patterns, wide_re, wide_im, measured,
    rim_send, rim_recv, scan_send, scan_recv, own_sem,
):
    ty, tx = lax.axis_index("ty"), lax.axis_index("tx")
    height, width = obj_re.shape
    extent = patterns.shape[1]
    blocks = width // LANES
    capacity = patterns.shape[0] // n_tx
    up, down = lax.rem(ty + n_ty - 1, n_ty), lax.rem(ty + 1, n_ty)
    left, right = lax.rem(tx + n_tx - 1, n_tx), lax.rem(tx + 1, n_tx)
    peers = [lax.rem(tx + d, n_tx) for d in range(1, n_tx)]
    greet(
        [(ty, p) for p in peers]
        + [(up, tx), (down, tx), (up, left), (down, right)]
    )
    rims = []
    for plane, (obj, wide) in enumerate(((obj_re, wide_re), (obj_im, wide_im))):
        base = plane * (blocks + 2)
        top = pl.ds(0, extent)
        below = pl.ds(height, extent)
        rims.append((
            obj.at[:, pl.ds(0, LANES)], wide.at[blocks, pl.ds(0, height), :], base,
            (ty, left), tx > 0, tx < n_tx - 1,
        ))
        for b in range(blocks):
            rims.append((
                obj.at[top, pl.ds(b * LANES, LANES)], wide.at[b, below, :], base + 1 + b,
                (up, tx), ty > 0, ty < n_ty - 1,
            ))
        rims.append((
            obj.at[top, pl.ds(0, LANES)], wide.at[blocks, below, :], base + 1 + blocks,
            (up, left), jnp.logical_and(tx > 0, ty > 0),
            jnp.logical_and(tx < n_tx - 1, ty < n_ty - 1),
        ))

    for src, dst, sem, partner, sends, takes in rims:
        @pl.when(sends)
        def _():
            remote(src, dst, rim_send.at[sem], rim_recv.at[sem], partner).start()

    def scan_copy(d):
        peer = peers[d - 1]
        return remote(
            patterns.at[pl.ds(peer * capacity, capacity)],
            measured.at[pl.ds(tx * capacity, capacity)],
            scan_send.at[d - 1], scan_recv.at[d - 1], (ty, peer),
        )

    for d in range(1, n_tx):
        scan_copy(d).start()
    own = pl.ds(tx * capacity, capacity)
    own_copy = pltpu.make_async_copy(patterns.at[own], measured.at[own], own_sem)
    own_copy.start()
    for obj, wide in ((obj_re, wide_re), (obj_im, wide_im)):
        for b in range(blocks):
            wide[b, :height, :] = obj[:, b * LANES : (b + 1) * LANES]
        for dst, absent in (
            (wide.at[blocks, pl.ds(0, height), :], tx == n_tx - 1),
            (wide.at[pl.ds(0, blocks), pl.ds(height, extent), :], ty == n_ty - 1),
            (
                wide.at[blocks, pl.ds(height, extent), :],
                jnp.logical_or(tx == n_tx - 1, ty == n_ty - 1),
            ),
        ):
            @pl.when(absent)
            def _():
                dst[...] = jnp.zeros(dst.shape, F32)

    own_copy.wait()
    for src, dst, sem, partner, sends, takes in rims:
        @pl.when(sends)
        def _():
            remote(src, dst, rim_send.at[sem], rim_recv.at[sem], partner).wait_send()

        @pl.when(takes)
        def _():
            remote(src, dst, rim_send.at[sem], rim_recv.at[sem], partner).wait_recv()

    for d in range(1, n_tx):
        source = lax.rem(tx + n_tx - d, n_tx)
        scan_copy(d).wait_send()
        remote(
            patterns.at[pl.ds(source * capacity, capacity)],
            measured.at[pl.ds(source * capacity, capacity)],
            scan_send.at[d - 1], scan_recv.at[d - 1], (ty, source),
        ).wait_recv()


def first_exchange(n_ty, n_tx, obj_re, obj_im, patterns):
    height, width = obj_re.shape
    extent = patterns.shape[1]
    blocks = width // LANES
    vmem = pl.BlockSpec(memory_space=pltpu.VMEM)
    wide = jax.ShapeDtypeStruct((blocks + 1, height + extent, LANES), F32)
    count = 2 * (blocks + 2)
    return pl.pallas_call(
        lambda *refs: first_exchange_kernel(n_ty, n_tx, *refs),
        out_shape=(wide, wide, jax.ShapeDtypeStruct(patterns.shape, F32)),
        in_specs=[vmem] * 3,
        out_specs=(vmem,) * 3,
        scratch_shapes=[
            pltpu.SemaphoreType.DMA((count,)),
            pltpu.SemaphoreType.DMA((count,)),
            pltpu.SemaphoreType.DMA((n_tx - 1,)),
            pltpu.SemaphoreType.DMA((n_tx - 1,)),
            pltpu.SemaphoreType.DMA,
        ],
        compiler_params=pltpu.CompilerParams(
            collective_id=0, has_side_effects=True, vmem_limit_bytes=48 * 1024 * 1024
        ),
        name="comm_first",
    )(obj_re, obj_im, patterns)


def stages_of(n_ty, n_tx):
    wanted = [("ty", 1, 2), ("ty", 2, n_ty // 2), ("tx", 1, 2), ("tx", 2, n_tx // 2)]
    return [stage for stage in wanted if stage[2] > 1]


def last_exchange_kernel(
    n_ty, n_tx, modes, numer, grads, obj_re, obj_im, probe_re, probe_im,
    new_re, new_im, new_probe_re, new_probe_im,
    beside, below, corner, result, halo_send, halo_recv, *scratch,
):
    stages = stages_of(n_ty, n_tx)
    depth = len(stages)
    received = scratch[:depth]
    partial = scratch[depth : 2 * depth - 1]
    send_sems, recv_sems, back_send, back_recv = scratch[2 * depth - 1 :]
    ty, tx = lax.axis_index("ty"), lax.axis_index("tx")
    height, width = obj_re.shape
    extent = probe_re.shape[1]
    blocks = width // LANES
    up, down = lax.rem(ty + n_ty - 1, n_ty), lax.rem(ty + 1, n_ty)
    left, right = lax.rem(tx + n_tx - 1, n_tx), lax.rem(tx + 1, n_tx)

    def member(stage):
        axis, stride, size = stage
        return lax.rem((ty if axis == "ty" else tx) // stride, size)

    def peer(stage, shift):
        axis, stride, size = stage
        q = member(stage)
        other = lax.rem(q + shift + size, size)
        if axis == "ty":
            return other, (ty + (other - q) * stride, tx)
        return other, (ty, tx + (other - q) * stride)

    partners = [(ty, left), (ty, right), (up, tx), (down, tx), (up, left), (down, right)]
    for stage in stages:
        for d in range(1, stage[2]):
            partners.append(peer(stage, d)[1])
    greet(partners)

    halos = (
        (numer.at[:, blocks, pl.ds(0, height), :], beside, 0, (ty, right),
         tx < n_tx - 1, tx > 0),
        (numer.at[:, pl.ds(0, blocks), pl.ds(height, extent), :], below, 1, (down, tx),
         ty < n_ty - 1, ty > 0),
        (numer.at[:, blocks, pl.ds(height, extent), :], corner, 2, (down, right),
         jnp.logical_and(tx < n_tx - 1, ty < n_ty - 1), jnp.logical_and(tx > 0, ty > 0)),
    )

    def halo_copy(halo):
        src, dst, sem, partner = halo[:4]
        return remote(src, dst, halo_send.at[sem], halo_recv.at[sem], partner)

    def start_halos(chosen):
        for halo in chosen:
            @pl.when(halo[4])
            def _():
                halo_copy(halo).start()

    power = probe_re[0] * probe_re[0] + probe_im[0] * probe_im[0]
    for m in range(1, modes):
        power = power + probe_re[m] * probe_re[m] + probe_im[m] * probe_im[m]
    floor = 0.1 * jnp.max(power)

    def update_object(b, r):
        cols = slice(b * LANES, (b + 1) * LANES)
        band = slice(r, r + extent)
        sums = []
        for plane in range(3):
            value = numer[plane, b, band, :]
            if r == 0:
                value = value + below[plane, b]
            if b == 0:
                value = value + beside[plane, band, :]
            if r == 0 and b == 0:
                value = value + corner[plane]
            sums.append(value)
        weight = sums[2] + floor
        new_re[band, cols] = obj_re[band, cols] + sums[0] / weight
        new_im[band, cols] = obj_im[band, cols] + sums[1] / weight

    rows = grads.shape[0]
    lengths = [rows]
    for stage in stages:
        lengths.append(lengths[-1] // stage[2])
    firsts = [0]
    while len(firsts) <= depth:
        firsts.append(firsts[-1] + (stages[len(firsts) - 1][2] - 1))
    source = grads
    base = jnp.int32(0)
    for s, stage in enumerate(stages):
        length = lengths[s + 1]
        copies = []
        for d in range(1, stage[2]):
            other, device = peer(stage, d)
            sem = firsts[s] + d - 1
            copies.append(remote(
                source.at[pl.ds(pl.multiple_of(other * length, 8), length), :],
                received[s].at[d - 1],
                send_sems.at[sem], recv_sems.at[sem], device,
            ))
        for copy in copies:
            copy.start()
        if s == 0:
            start_halos(halos[:1])
        if s == 1:
            for b in range(1, blocks):
                for r in range(extent, height, extent):
                    update_object(b, r)
        for copy in copies:
            copy.wait()
        if s == 1:
            start_halos(halos[1:])
        q = member(stage)
        total = source[pl.ds(pl.multiple_of(q * length, 8), length), :]
        for d in range(1, stage[2]):
            total = total + received[s][d - 1]
        base = base + q * length
        if s < depth - 1:
            source = partial[s]
            source[...] = total
        else:
            result[pl.ds(pl.multiple_of(base, 8), length), :] = total
    pending = []
    for s in range(depth - 1, -1, -1):
        stage, length = stages[s], lengths[s + 1]
        held = result.at[pl.ds(pl.multiple_of(base, 8), length), :]
        copies = []
        for d in range(1, stage[2]):
            other, device = peer(stage, d)
            sem = firsts[s] + d - 1
            copy = remote(held, held, back_send.at[sem], back_recv.at[sem], device)
            copy.start()
            copies.append(copy)
        q = member(stage)
        for d in range(1, stage[2]):
            other, device = peer(stage, -d)
            sem = firsts[s] + d - 1
            place = result.at[pl.ds(pl.multiple_of(base + (other - q) * length, 8), length), :]
            remote(place, place, back_send.at[sem], back_recv.at[sem], device).wait_recv()
        pending += copies
        base = base - q * length
    for copy in pending:
        copy.wait_send()

    norm = result[pl.ds(2 * modes * extent, extent), :] + 1.0
    for m in range(modes):
        real = result[pl.ds(m * extent, extent), :]
        imag = result[pl.ds((modes + m) * extent, extent), :]
        new_probe_re[m] = probe_re[m] + real / norm
        new_probe_im[m] = probe_im[m] + imag / norm

    for halo in halos:
        @pl.when(halo[4])
        def _():
            halo_copy(halo).wait_send()

        @pl.when(halo[5])
        def _():
            halo_copy(halo).wait_recv()

    for halo in halos:
        @pl.when(jnp.logical_not(halo[5]))
        def _():
            halo[1][...] = jnp.zeros(halo[1].shape, F32)

    for b in range(blocks):
        for r in range(0, height, extent):
            if b == 0 or r == 0:
                update_object(b, r)


def last_exchange(n_ty, n_tx, numer, grads, obj_re, obj_im, probe_re, probe_im):
    modes, extent = probe_re.shape[0], probe_re.shape[1]
    height, width = obj_re.shape
    blocks = width // LANES
    stages = stages_of(n_ty, n_tx)
    rows = grads.shape[0]
    vmem = pl.BlockSpec(memory_space=pltpu.VMEM)
    received, partial = [], []
    length = rows
    for stage in stages:
        length = length // stage[2]
        received.append(pltpu.VMEM((stage[2] - 1, length, LANES), F32))
        partial.append(pltpu.VMEM((length, LANES), F32))
    count = sum(stage[2] - 1 for stage in stages)
    tile = jax.ShapeDtypeStruct(obj_re.shape, F32)
    wave = jax.ShapeDtypeStruct(probe_re.shape, F32)
    return pl.pallas_call(
        lambda *refs: last_exchange_kernel(n_ty, n_tx, modes, *refs),
        out_shape=(tile, tile, wave, wave),
        in_specs=[vmem] * 6,
        out_specs=(vmem,) * 4,
        scratch_shapes=[
            pltpu.VMEM((3, height, LANES), F32),
            pltpu.VMEM((3, blocks, extent, LANES), F32),
            pltpu.VMEM((3, extent, LANES), F32),
            pltpu.VMEM((rows, LANES), F32),
            pltpu.SemaphoreType.DMA((3,)),
            pltpu.SemaphoreType.DMA((3,)),
            *received,
            *partial[:-1],
            *[pltpu.SemaphoreType.DMA((count,))] * 4,
        ],
        compiler_params=pltpu.CompilerParams(
            collective_id=1, has_side_effects=True, vmem_limit_bytes=48 * 1024 * 1024
        ),
        name="comm_last",
    )(numer, grads, obj_re, obj_im, probe_re, probe_im)


def body(object_re, object_im, probe_re, probe_im, patterns, offsets, counts):
    n_ty, n_tx = lax.axis_size("ty"), lax.axis_size("tx")
    modes, extent = probe_re.shape[0], probe_re.shape[1]
    wide_re, wide_im, measured = first_exchange(n_ty, n_tx, object_re, object_im, patterns[0, 0])
    rows = (2 * modes + 1) * extent
    unit = 8 * n_ty * n_tx
    unit = unit * extent // math.gcd(unit, extent)
    grad_planes = -(-rows // unit) * unit // extent
    numer, grads = local_work(
        offsets[0, 0], counts[0, 0], wide_re, wide_im, probe_re, probe_im, measured, grad_planes
    )
    return last_exchange(
        n_ty, n_tx, numer, grads.reshape(grad_planes * extent, extent),
        object_re, object_im, probe_re, probe_im,
    )


def solution(mesh):
    return jax.shard_map(
        body,
        mesh=mesh,
        in_specs=(
            P("ty", "tx"),
            P("ty", "tx"),
            P(),
            P(),
            P("ty", "tx", None, None, None),
            P("ty", "tx", None, None),
            P("ty", "tx", None),
        ),
        out_specs=(P("ty", "tx"), P("ty", "tx"), P(), P()),
        check_vma=False,
    )
```

```python
import math

import jax
import jax.numpy as jnp
import ml_dtypes
import numpy as np
from jax import lax
from jax.experimental import pallas as pl
from jax.experimental.pallas import tpu as pltpu
from jax.sharding import PartitionSpec as P

BF16 = jnp.bfloat16
F32 = jnp.float32
LANES = 128


def dft_tables(extent):
    k = np.arange(extent)
    angle = (k[:, None] * k[None, :] % extent) * (-2.0 * math.pi / extent)
    cos, sin = np.cos(angle) / math.sqrt(extent), np.sin(angle) / math.sqrt(extent)
    table = np.block([[cos, sin], [-sin, cos]])

    def parts(values):
        high = values.astype(np.float32).astype(ml_dtypes.bfloat16)
        low = (values - high.astype(np.float64)).astype(np.float32).astype(ml_dtypes.bfloat16)
        return high, low

    high, low = parts(table)
    flip_high, flip_low = parts(table.T)
    return (
        np.concatenate([high, high, low], axis=0),
        np.concatenate([flip_high, flip_high, flip_low], axis=1),
        np.concatenate([high, high, low], axis=1),
        np.concatenate([flip_high, flip_high, flip_low], axis=0),
    )


def split(value):
    high = value.astype(BF16)
    low = (value - high.astype(F32)).astype(BF16)
    return high, low


def right_product(real, imag, table):
    rh, rl = split(real)
    ih, il = split(imag)
    lhs = jnp.concatenate([rh, ih, rl, il, rh, ih], axis=1)
    return jnp.dot(lhs, table, preferred_element_type=F32)


def left_product(table, real, imag):
    rh, rl = split(real)
    ih, il = split(imag)
    rhs = jnp.concatenate([rh, ih, rl, il, rh, ih], axis=0)
    return jnp.dot(table, rhs, preferred_element_type=F32)


def main_kernel(
    offsets, counts, wide_re, wide_im, probe_re, probe_im, measured,
    right_fwd, left_fwd, left_inv, right_inv,
    numer, grads,
    patch, power, far,
):
    slots, extent = measured.shape[0], measured.shape[1]
    modes = probe_re.shape[0]
    capacity = slots // counts.shape[0]
    numer[...] = jnp.zeros_like(numer)
    grads[...] = jnp.zeros_like(grads)
    lane = lax.broadcasted_iota(jnp.int32, (extent, LANES), 1)
    summed = probe_re[0] * probe_re[0] + probe_im[0] * probe_im[0]
    for m in range(1, modes):
        summed = summed + probe_re[m] * probe_re[m] + probe_im[m] * probe_im[m]
    power[...] = summed

    def visit(slot, carry):
        alive = slot % capacity < counts[slot // capacity]

        @pl.when(alive)
        def _():
            row = offsets[slot, 0]
            col = offsets[slot, 1]
            block = col // LANES
            inner = col % LANES
            rows = pl.ds(row, extent)
            back = lax.rem(LANES - inner, LANES)

            def cut(wide):
                first = pltpu.roll(wide[block, rows, :], back, 1)
                second = pltpu.roll(wide[block + 1, rows, :], back, 1)
                return jnp.where(lane < LANES - inner, first, second)

            patch[0] = cut(wide_re)
            patch[1] = cut(wide_im)
            total = jnp.zeros((extent, extent), F32)
            for m in range(0, modes, 2):
                mids = []
                for n in (m, m + 1):
                    a, b = patch[0], patch[1]
                    p, q = probe_re[n], probe_im[n]
                    mids.append(right_product(p * a - q * b, p * b + q * a, right_fwd[...]))
                wide_real = jnp.concatenate([y[:, :extent] for y in mids], axis=1)
                wide_imag = jnp.concatenate([y[:, extent:] for y in mids], axis=1)
                z = left_product(left_fwd[...], wide_real, wide_imag)
                far[m // 2] = z
                s = z[:extent] * z[:extent] + z[extent:] * z[extent:]
                total = total + s[:, :extent] + s[:, extent:]
            factor = jnp.sqrt(measured[slot]) / jnp.sqrt(jnp.maximum(total, 1.0)) - 1.0
            both = jnp.concatenate([factor, factor], axis=1)
            up_re = jnp.zeros((extent, extent), F32)
            up_im = jnp.zeros((extent, extent), F32)
            for m in range(0, modes, 2):
                z = far[m // 2]
                g = left_product(left_inv[...], z[:extent] * both, z[extent:] * both)
                for n in (m, m + 1):
                    cut_n = slice((n - m) * extent, (n - m + 1) * extent)
                    chi = right_product(g[:extent, cut_n], g[extent:, cut_n], right_inv[...])
                    c, d = chi[:, :extent], chi[:, extent:]
                    a, b = patch[0], patch[1]
                    p, q = probe_re[n], probe_im[n]
                    up_re = up_re + p * c + q * d
                    up_im = up_im + p * d - q * c
                    grads[n] += a * c + b * d
                    grads[modes + n] += a * d - b * c
            a, b = patch[0], patch[1]
            grads[2 * modes] += a * a + b * b

            def place(plane, piece):
                moved = pltpu.roll(piece, inner, 1)
                numer[plane, block, rows, :] += jnp.where(lane >= inner, moved, 0.0)
                numer[plane, block + 1, rows, :] += jnp.where(lane < inner, moved, 0.0)

            place(0, up_re)
            place(1, up_im)
            place(2, power[...])

        return carry

    lax.fori_loop(0, slots, visit, 0)


def local_work(
    offsets, counts, wide_re, wide_im, probe_re, probe_im, measured, grad_planes
):
    modes, extent = probe_re.shape[0], probe_re.shape[1]
    tables = dft_tables(extent)
    vmem = pl.BlockSpec(memory_space=pltpu.VMEM)
    smem = pl.BlockSpec(memory_space=pltpu.SMEM)
    return pl.pallas_call(
        main_kernel,
        out_shape=(
            jax.ShapeDtypeStruct((3,) + wide_re.shape, F32),
            jax.ShapeDtypeStruct((grad_planes, extent, extent), F32),
        ),
        in_specs=[smem, smem] + [vmem] * 9,
        out_specs=(vmem,) * 2,
        scratch_shapes=[
            pltpu.VMEM((2, extent, extent), F32),
            pltpu.VMEM((extent, extent), F32),
            pltpu.VMEM((modes // 2, 2 * extent, 2 * extent), F32),
        ],
        compiler_params=pltpu.CompilerParams(vmem_limit_bytes=48 * 1024 * 1024),
        name="local_work",
    )(offsets, counts, wide_re, wide_im, probe_re, probe_im, measured, *tables)


def greet(partners):
    barrier = pltpu.get_barrier_semaphore()
    for partner in partners:
        pl.semaphore_signal(barrier, inc=1, device_id=partner, device_id_type=pl.DeviceIdType.MESH)
    pl.semaphore_wait(barrier, len(partners))


def remote(src, dst, send, recv, partner):
    return pltpu.make_async_remote_copy(
        src_ref=src, dst_ref=dst, send_sem=send, recv_sem=recv,
        device_id=partner, device_id_type=pl.DeviceIdType.MESH,
    )


def first_exchange_kernel(
    n_ty, n_tx, obj_re, obj_im, patterns, wide_re, wide_im, measured,
    rim_send, rim_recv, scan_send, scan_recv, own_sem,
):
    ty, tx = lax.axis_index("ty"), lax.axis_index("tx")
    height, width = obj_re.shape
    extent = patterns.shape[1]
    blocks = width // LANES
    capacity = patterns.shape[0] // n_tx
    up, down = lax.rem(ty + n_ty - 1, n_ty), lax.rem(ty + 1, n_ty)
    left, right = lax.rem(tx + n_tx - 1, n_tx), lax.rem(tx + 1, n_tx)
    peers = [lax.rem(tx + d, n_tx) for d in range(1, n_tx)]
    greet(
        [(ty, p) for p in peers]
        + [(up, tx), (down, tx), (up, left), (down, right)]
    )
    rims = []
    for plane, (obj, wide) in enumerate(((obj_re, wide_re), (obj_im, wide_im))):
        base = plane * (blocks + 2)
        top = pl.ds(0, extent)
        below = pl.ds(height, extent)
        rims.append((
            obj.at[:, pl.ds(0, LANES)], wide.at[blocks, pl.ds(0, height), :], base,
            (ty, left), tx > 0, tx < n_tx - 1,
        ))
        for b in range(blocks):
            rims.append((
                obj.at[top, pl.ds(b * LANES, LANES)], wide.at[b, below, :], base + 1 + b,
                (up, tx), ty > 0, ty < n_ty - 1,
            ))
        rims.append((
            obj.at[top, pl.ds(0, LANES)], wide.at[blocks, below, :], base + 1 + blocks,
            (up, left), jnp.logical_and(tx > 0, ty > 0),
            jnp.logical_and(tx < n_tx - 1, ty < n_ty - 1),
        ))

    def scan_copy(d):
        peer = peers[d - 1]
        return remote(
            patterns.at[pl.ds(peer * capacity, capacity)],
            measured.at[pl.ds(tx * capacity, capacity)],
            scan_send.at[d - 1], scan_recv.at[d - 1], (ty, peer),
        )

    for d in range(1, n_tx):
        scan_copy(d).start()

    for src, dst, sem, partner, sends, takes in rims:
        @pl.when(sends)
        def _():
            remote(src, dst, rim_send.at[sem], rim_recv.at[sem], partner).start()

    own = pl.ds(tx * capacity, capacity)
    own_copy = pltpu.make_async_copy(patterns.at[own], measured.at[own], own_sem)
    own_copy.start()
    for obj, wide in ((obj_re, wide_re), (obj_im, wide_im)):
        for b in range(blocks):
            wide[b, :height, :] = obj[:, b * LANES : (b + 1) * LANES]
        for dst, absent in (
            (wide.at[blocks, pl.ds(0, height), :], tx == n_tx - 1),
            (wide.at[pl.ds(0, blocks), pl.ds(height, extent), :], ty == n_ty - 1),
            (
                wide.at[blocks, pl.ds(height, extent), :],
                jnp.logical_or(tx == n_tx - 1, ty == n_ty - 1),
            ),
        ):
            @pl.when(absent)
            def _():
                dst[...] = jnp.zeros(dst.shape, F32)

    own_copy.wait()
    for src, dst, sem, partner, sends, takes in rims:
        @pl.when(sends)
        def _():
            remote(src, dst, rim_send.at[sem], rim_recv.at[sem], partner).wait_send()

        @pl.when(takes)
        def _():
            remote(src, dst, rim_send.at[sem], rim_recv.at[sem], partner).wait_recv()

    for d in range(1, n_tx):
        source = lax.rem(tx + n_tx - d, n_tx)
        scan_copy(d).wait_send()
        remote(
            patterns.at[pl.ds(source * capacity, capacity)],
            measured.at[pl.ds(source * capacity, capacity)],
            scan_send.at[d - 1], scan_recv.at[d - 1], (ty, source),
        ).wait_recv()


def first_exchange(n_ty, n_tx, obj_re, obj_im, patterns):
    height, width = obj_re.shape
    extent = patterns.shape[1]
    blocks = width // LANES
    vmem = pl.BlockSpec(memory_space=pltpu.VMEM)
    wide = jax.ShapeDtypeStruct((blocks + 1, height + extent, LANES), F32)
    count = 2 * (blocks + 2)
    return pl.pallas_call(
        lambda *refs: first_exchange_kernel(n_ty, n_tx, *refs),
        out_shape=(wide, wide, jax.ShapeDtypeStruct(patterns.shape, F32)),
        in_specs=[vmem] * 3,
        out_specs=(vmem,) * 3,
        scratch_shapes=[
            pltpu.SemaphoreType.DMA((count,)),
            pltpu.SemaphoreType.DMA((count,)),
            pltpu.SemaphoreType.DMA((n_tx - 1,)),
            pltpu.SemaphoreType.DMA((n_tx - 1,)),
            pltpu.SemaphoreType.DMA,
        ],
        compiler_params=pltpu.CompilerParams(
            collective_id=0, has_side_effects=True, vmem_limit_bytes=48 * 1024 * 1024
        ),
        name="comm_first",
    )(obj_re, obj_im, patterns)


def stages_of(n_ty, n_tx):
    wanted = [("ty", 1, 2), ("ty", 2, n_ty // 2), ("tx", 1, 2), ("tx", 2, n_tx // 2)]
    return [stage for stage in wanted if stage[2] > 1]


def last_exchange_kernel(
    n_ty, n_tx, modes, numer, grads, obj_re, obj_im, probe_re, probe_im,
    new_re, new_im, new_probe_re, new_probe_im,
    beside, below, corner, result, halo_send, halo_recv, *scratch,
):
    stages = stages_of(n_ty, n_tx)
    depth = len(stages)
    received = scratch[:depth]
    partial = scratch[depth : 2 * depth - 1]
    send_sems, recv_sems, back_send, back_recv = scratch[2 * depth - 1 :]
    ty, tx = lax.axis_index("ty"), lax.axis_index("tx")
    height, width = obj_re.shape
    extent = probe_re.shape[1]
    blocks = width // LANES
    up, down = lax.rem(ty + n_ty - 1, n_ty), lax.rem(ty + 1, n_ty)
    left, right = lax.rem(tx + n_tx - 1, n_tx), lax.rem(tx + 1, n_tx)

    def member(stage):
        axis, stride, size = stage
        return lax.rem((ty if axis == "ty" else tx) // stride, size)

    def peer(stage, shift):
        axis, stride, size = stage
        q = member(stage)
        other = lax.rem(q + shift + size, size)
        if axis == "ty":
            return other, (ty + (other - q) * stride, tx)
        return other, (ty, tx + (other - q) * stride)

    partners = [(ty, left), (ty, right), (up, tx), (down, tx), (up, left), (down, right)]
    for stage in stages:
        for d in range(1, stage[2]):
            partners.append(peer(stage, d)[1])
    greet(partners)

    halos = (
        (numer.at[:, blocks, pl.ds(0, height), :], beside, 0, (ty, right),
         tx < n_tx - 1, tx > 0),
        (numer.at[:, pl.ds(0, blocks), pl.ds(height, extent), :], below, 1, (down, tx),
         ty < n_ty - 1, ty > 0),
        (numer.at[:, blocks, pl.ds(height, extent), :], corner, 2, (down, right),
         jnp.logical_and(tx < n_tx - 1, ty < n_ty - 1), jnp.logical_and(tx > 0, ty > 0)),
    )

    def halo_copy(halo):
        src, dst, sem, partner = halo[:4]
        return remote(src, dst, halo_send.at[sem], halo_recv.at[sem], partner)

    def start_halos(chosen):
        for halo in chosen:
            @pl.when(halo[4])
            def _():
                halo_copy(halo).start()

    power = probe_re[0] * probe_re[0] + probe_im[0] * probe_im[0]
    for m in range(1, modes):
        power = power + probe_re[m] * probe_re[m] + probe_im[m] * probe_im[m]
    floor = 0.1 * jnp.max(power)

    def update_object(b, r):
        cols = slice(b * LANES, (b + 1) * LANES)
        band = slice(r, r + extent)
        sums = []
        for plane in range(3):
            value = numer[plane, b, band, :]
            if r == 0:
                value = value + below[plane, b]
            if b == 0:
                value = value + beside[plane, band, :]
            if r == 0 and b == 0:
                value = value + corner[plane]
            sums.append(value)
        weight = sums[2] + floor
        new_re[band, cols] = obj_re[band, cols] + sums[0] / weight
        new_im[band, cols] = obj_im[band, cols] + sums[1] / weight

    rows = grads.shape[0]
    lengths = [rows]
    for stage in stages:
        lengths.append(lengths[-1] // stage[2])
    firsts = [0]
    while len(firsts) <= depth:
        firsts.append(firsts[-1] + (stages[len(firsts) - 1][2] - 1))
    source = grads
    base = jnp.int32(0)
    for s, stage in enumerate(stages):
        length = lengths[s + 1]
        copies = []
        for d in range(1, stage[2]):
            other, device = peer(stage, d)
            sem = firsts[s] + d - 1
            copies.append(remote(
                source.at[pl.ds(pl.multiple_of(other * length, 8), length), :],
                received[s].at[d - 1],
                send_sems.at[sem], recv_sems.at[sem], device,
            ))
        for copy in copies:
            copy.start()
        if s == 0:
            start_halos(halos[:1])
        if s == 1:
            for b in range(1, blocks):
                for r in range(extent, height, extent):
                    update_object(b, r)
        for copy in copies:
            copy.wait()
        if s == 1:
            start_halos(halos[1:])
        q = member(stage)
        total = source[pl.ds(pl.multiple_of(q * length, 8), length), :]
        for d in range(1, stage[2]):
            total = total + received[s][d - 1]
        base = base + q * length
        if s < depth - 1:
            source = partial[s]
            source[...] = total
        else:
            result[pl.ds(pl.multiple_of(base, 8), length), :] = total
    pending = []
    for s in range(depth - 1, -1, -1):
        stage, length = stages[s], lengths[s + 1]
        held = result.at[pl.ds(pl.multiple_of(base, 8), length), :]
        copies = []
        for d in range(1, stage[2]):
            other, device = peer(stage, d)
            sem = firsts[s] + d - 1
            copy = remote(held, held, back_send.at[sem], back_recv.at[sem], device)
            copy.start()
            copies.append(copy)
        q = member(stage)
        for d in range(1, stage[2]):
            other, device = peer(stage, -d)
            sem = firsts[s] + d - 1
            place = result.at[pl.ds(pl.multiple_of(base + (other - q) * length, 8), length), :]
            remote(place, place, back_send.at[sem], back_recv.at[sem], device).wait_recv()
        pending += copies
        base = base - q * length
    for copy in pending:
        copy.wait_send()

    norm = result[pl.ds(2 * modes * extent, extent), :] + 1.0
    for m in range(modes):
        real = result[pl.ds(m * extent, extent), :]
        imag = result[pl.ds((modes + m) * extent, extent), :]
        new_probe_re[m] = probe_re[m] + real / norm
        new_probe_im[m] = probe_im[m] + imag / norm

    for halo in halos:
        @pl.when(halo[4])
        def _():
            halo_copy(halo).wait_send()

        @pl.when(halo[5])
        def _():
            halo_copy(halo).wait_recv()

    for halo in halos:
        @pl.when(jnp.logical_not(halo[5]))
        def _():
            halo[1][...] = jnp.zeros(halo[1].shape, F32)

    for b in range(blocks):
        for r in range(0, height, extent):
            if b == 0 or r == 0:
                update_object(b, r)


def last_exchange(n_ty, n_tx, numer, grads, obj_re, obj_im, probe_re, probe_im):
    modes, extent = probe_re.shape[0], probe_re.shape[1]
    height, width = obj_re.shape
    blocks = width // LANES
    stages = stages_of(n_ty, n_tx)
    rows = grads.shape[0]
    vmem = pl.BlockSpec(memory_space=pltpu.VMEM)
    received, partial = [], []
    length = rows
    for stage in stages:
        length = length // stage[2]
        received.append(pltpu.VMEM((stage[2] - 1, length, LANES), F32))
        partial.append(pltpu.VMEM((length, LANES), F32))
    count = sum(stage[2] - 1 for stage in stages)
    tile = jax.ShapeDtypeStruct(obj_re.shape, F32)
    wave = jax.ShapeDtypeStruct(probe_re.shape, F32)
    return pl.pallas_call(
        lambda *refs: last_exchange_kernel(n_ty, n_tx, modes, *refs),
        out_shape=(tile, tile, wave, wave),
        in_specs=[vmem] * 6,
        out_specs=(vmem,) * 4,
        scratch_shapes=[
            pltpu.VMEM((3, height, LANES), F32),
            pltpu.VMEM((3, blocks, extent, LANES), F32),
            pltpu.VMEM((3, extent, LANES), F32),
            pltpu.VMEM((rows, LANES), F32),
            pltpu.SemaphoreType.DMA((3,)),
            pltpu.SemaphoreType.DMA((3,)),
            *received,
            *partial[:-1],
            *[pltpu.SemaphoreType.DMA((count,))] * 4,
        ],
        compiler_params=pltpu.CompilerParams(
            collective_id=1, has_side_effects=True, vmem_limit_bytes=48 * 1024 * 1024
        ),
        name="comm_last",
    )(numer, grads, obj_re, obj_im, probe_re, probe_im)


def body(object_re, object_im, probe_re, probe_im, patterns, offsets, counts):
    n_ty, n_tx = lax.axis_size("ty"), lax.axis_size("tx")
    modes, extent = probe_re.shape[0], probe_re.shape[1]
    wide_re, wide_im, measured = first_exchange(n_ty, n_tx, object_re, object_im, patterns[0, 0])
    rows = (2 * modes + 1) * extent
    unit = 8 * n_ty * n_tx
    unit = unit * extent // math.gcd(unit, extent)
    grad_planes = -(-rows // unit) * unit // extent
    numer, grads = local_work(
        offsets[0, 0], counts[0, 0], wide_re, wide_im, probe_re, probe_im, measured, grad_planes
    )
    return last_exchange(
        n_ty, n_tx, numer, grads.reshape(grad_planes * extent, extent),
        object_re, object_im, probe_re, probe_im,
    )


def solution(mesh):
    return jax.shard_map(
        body,
        mesh=mesh,
        in_specs=(
            P("ty", "tx"),
            P("ty", "tx"),
            P(),
            P(),
            P("ty", "tx", None, None, None),
            P("ty", "tx", None, None),
            P("ty", "tx", None),
        ),
        out_specs=(P("ty", "tx"), P("ty", "tx"), P(), P()),
        check_vma=False,
    )
```
